512 devices in a mesh: seq: 16 (over x_hi, y), group: 32 (over z, x_lo, core).
Axes of the slice: x: 4 (x_hi: 2, x_lo: 2; x = x_hi * 2 + x_lo), y: 8, z: 8, core: 2. Of those that a mesh axis runs over, the one named last changes fastest.
Arguments:
- query_proj: bfloat16 [32, 1024, 8192], P('group', 'seq'), may hold values from -6 to 6
- key_proj: bfloat16 [32, 1024, 1024], P('group', 'seq'), may hold values from -6 to 6
- value_proj: bfloat16 [32, 1024, 1024], P('group', 'seq'), may hold values from -6 to 6
- query_gain: float32 [128], replicated, may hold values from 1 to 5.5, as said below
- key_gain: float32 [128], replicated, may hold values from 1 to 5.5, as said below
- doc_lengths: int32 [32, 4], P('group'), may hold values from 1 to 512, 1024 in all within a row
Outputs:
- attended: bfloat16 [32, 1024, 8192], P('group', 'seq')
- cache: bfloat16 [16, 32, 32, 1, 16, 256], P('seq', 'group')
The draws below stay inside these ranges and needn't reach their ends.
Inputs may be any that keep to these rules, and one draw needn't show every extreme that they name: `query_gain`: a gain for each of the 128 features. `key_gain`: a gain for each of the 128 features.
All inputs are finite; a program needn't handle non-finite values.
Results may differ from the reference program's by a relative error of at most 0.0045.
The reference program's roundings to bfloat16 on the way count: a program that leaves them out, or rounds other values in their place, can miss the bound.
Values may be sent and summed in bfloat16 or wider, within the bound.
No kernel may reach another device: no remote copies, remote signals or barrier semaphores. Data moves between devices by JAX's collectives and lax.ppermute only.
A program may use at most 64 MiB of HBM per device.

```python
import math
import jax
import jax.numpy as jnp
import numpy as np
from jax import lax

HQ = 64
KVH = 8
HD = 128
PAGE = 16
DOCS = 4
PROMPTS = 32
SEQ_LEN = 1024
MOST = 512
KR = 16
REP = 2
PAGES_DEV = 1
N_GROUP = 32


def draw_query_gain(key, part):
    key = jax.random.fold_in(key, 11)
    return jnp.exp(jax.random.uniform(key, (HD,), jnp.float32, 0.0, math.log(3.0)))


def draw_key_gain(key, part):
    key = jax.random.fold_in(key, 23)
    return jnp.exp(jax.random.uniform(key, (HD,), jnp.float32, 0.0, math.log(3.0)))


def block_scale(key, extent, split, smallest, high):
    def one(dim, shards_of):
        heights = jax.random.uniform(jax.random.fold_in(jax.random.fold_in(key, 6), dim), (shards_of,), jnp.float32, smallest / len(split), high / len(split))
        return jnp.repeat(jnp.exp(heights), extent[dim] // shards_of).reshape((-1,) + (1,) * (len(extent) - dim - 1))

    level = one(*split[0])
    for cut in split[1:]:
        level = level * one(*cut)
    return level


def profile(amount, total, reach, skew):
    weights = [(1 << 20) // math.isqrt(rank ** skew) + 1 for rank in range(2, amount + 1)]
    surplus, given = total - reach - (amount - 1), [1] * (amount - 1)
    while surplus > 0:
        movable = [i for i in range(amount - 1) if given[i] < reach]
        mass, remaining = sum([weights[i] for i in movable]), surplus
        for i in movable:
            more = min(reach - given[i], max(1, remaining * weights[i] // mass), surplus)
            given[i] = given[i] + more
            surplus = surplus - more
    return np.array([reach] + given)


def uneven_parts(key, count, total, reach, lean):
    if count == 2:
        one = jax.random.randint(key, (), max(1, total - reach), min(reach, total - 1) + 1)
        return jnp.stack([one, total - one])
    sizes = jnp.asarray(profile(count, total, reach, lean), jnp.int32)
    pairs = (count - 1) // 2
    giver, sink = sizes[1:1 + 2 * pairs:2], sizes[2:2 + 2 * pairs:2]
    room = jnp.minimum(giver - 1, reach - sink)
    moved = jax.random.randint(jax.random.fold_in(key, 1), (pairs,), 0, 1 << 20) % (room + 1)
    sizes = sizes.at[1:1 + 2 * pairs:2].set(giver - moved).at[2:2 + 2 * pairs:2].set(sink + moved)
    return sizes[jax.random.permutation(jax.random.fold_in(key, 2), count)]


def gaussian(rng, extent, deviation, most, shards=(), kind=jnp.bfloat16):
    drawn = deviation * jax.random.normal(rng, extent, jnp.float32)
    if shards:
        drawn = drawn * block_scale(rng, extent, shards, -0.22, 0.18)
    return jnp.clip(drawn, -most, most).astype(kind)


def setup_inputs(seed: int = 0) -> dict:
    keys = jax.random.split(jax.random.key(seed), 7)
    query_proj = gaussian(keys[0], (PROMPTS, SEQ_LEN, HQ * HD), 1.0, 6.0, ((0, 32), (1, 16)))
    key_proj = gaussian(keys[1], (PROMPTS, SEQ_LEN, KVH * HD), 1.0, 6.0, ((0, 32), (1, 16)))
    value_proj = gaussian(keys[2], (PROMPTS, SEQ_LEN, KVH * HD), 1.0, 6.0, ((0, 32), (1, 16)))
    query_gain = draw_query_gain(jax.random.fold_in(keys[6], 71), 0)
    key_gain = draw_key_gain(jax.random.fold_in(keys[6], 71), 0)
    doc_lengths = jax.vmap(lambda own: uneven_parts(own, DOCS, SEQ_LEN, MOST, 2))(jax.random.split(keys[5], PROMPTS)).reshape((PROMPTS, DOCS)).astype(jnp.int32)
    return dict(query_proj=query_proj, key_proj=key_proj, value_proj=value_proj, query_gain=query_gain, key_gain=key_gain, doc_lengths=doc_lengths)


NORM_EPS = 1e-06
ROPE_BASE = 1000000.0
MASKED = -1e+30

def token_starts(lengths, count):
    doc_ends = jnp.cumsum(lengths).astype(jnp.int32)
    token_index = jnp.arange(count, dtype=jnp.int32)
    passed = (doc_ends[None, :] <= token_index[:, None]).astype(jnp.int32)
    return lax.optimization_barrier(jnp.sum(passed * lengths[None, :], axis=1)).astype(jnp.int32)

def rope_tables(positions, head_width):
    half_width = head_width // 2
    exponent = jnp.arange(half_width, dtype=jnp.float32) * (-2.0 / head_width)
    inverse = jnp.power(jnp.float32(ROPE_BASE), exponent)
    angles = positions.astype(jnp.float32)[:, None] * inverse[None, :]
    return (jnp.cos(angles), jnp.sin(angles))

def norm_rope(heads_in, gain, cosine, sine):
    values_f = heads_in.astype(jnp.float32)
    inv_rms = lax.rsqrt(lax.optimization_barrier(jnp.mean(values_f * values_f, axis=-1, keepdims=True)) + NORM_EPS)
    normed = values_f * inv_rms * gain
    half_width = heads_in.shape[-1] // 2
    front = normed[..., :half_width]
    back_half = normed[..., half_width:]
    cos_b = cosine[:, None, :]
    sin_b = sine[:, None, :]
    rotated = jnp.concatenate([front * cos_b - back_half * sin_b, back_half * cos_b + front * sin_b], axis=-1)
    return rotated.astype(jnp.bfloat16)

def one_prompt(query_row, key_row, value_row, query_gain, key_gain, lengths):
    starts = token_starts(lengths, SEQ_LEN)
    token_index = jnp.arange(SEQ_LEN, dtype=jnp.int32)
    cosine, sine = rope_tables(token_index - starts, HD)
    q_rot = norm_rope(query_row.reshape(SEQ_LEN, HQ, HD), query_gain, cosine, sine)
    k_rot = norm_rope(key_row.reshape(SEQ_LEN, KVH, HD), key_gain, cosine, sine)
    values = value_row.reshape(SEQ_LEN, KVH, HD)
    visible = (token_index[None, :] <= token_index[:, None]) & (token_index[None, :] >= starts[:, None])
    grouped = q_rot.reshape(SEQ_LEN, KVH, HQ // KVH, HD)
    score_scale = 1.0 / math.sqrt(HD)

    def per_head(head_id):
        q_head = lax.dynamic_index_in_dim(grouped, head_id, 1, False).astype(jnp.float32)
        k_head = lax.dynamic_index_in_dim(k_rot, head_id, 1, False).astype(jnp.float32)
        v_head = lax.dynamic_index_in_dim(values, head_id, 1, False).astype(jnp.float32)
        scores = jnp.einsum('qgd,kd->gqk', q_head, k_head) * score_scale
        scores = jnp.where(visible[None], scores, MASKED)
        row_top = lax.optimization_barrier(jnp.max(scores, axis=-1, keepdims=True))
        weights = jnp.where(visible[None], jnp.exp(scores - row_top), 0.0)
        denom = lax.optimization_barrier(jnp.sum(weights, axis=-1, keepdims=True))
        rounded = lax.optimization_barrier(weights.astype(jnp.bfloat16)).astype(jnp.float32)
        mixed = jnp.einsum('gqk,kd->gqd', rounded, v_head)
        return (mixed / denom).astype(jnp.bfloat16)
    outputs = lax.map(per_head, jnp.arange(KVH, dtype=jnp.int32))
    attended = outputs.transpose(2, 0, 1, 3).reshape(SEQ_LEN, HQ * HD)
    pairs = jnp.concatenate([k_rot, values], axis=-1)
    return (attended, pairs)

def reference(query_proj, key_proj, value_proj, query_gain, key_gain, doc_lengths):

    def per_prompt(pieces):
        return one_prompt(pieces[0], pieces[1], pieces[2], query_gain, key_gain, pieces[3])
    attended, pairs = lax.map(per_prompt, (query_proj, key_proj, value_proj, doc_lengths))
    paged = pairs.reshape(PROMPTS, PAGES_DEV, REP, N_GROUP, PAGE, KVH, 2 * HD)
    cache = paged.transpose(5, 2, 3, 0, 1, 4, 6).reshape(KR, N_GROUP, PROMPTS, PAGES_DEV, PAGE, 2 * HD)
    return (attended, cache)
```

```python
import math

import jax
import jax.numpy as jnp
from jax import lax
from jax.experimental import pallas as pl
from jax.experimental.pallas import tpu as pltpu
from jax.sharding import PartitionSpec as P

PAGE = 16
NORM_EPS = 1e-06
ROPE_BASE = 1000000.0
MASKED = -1e30
HD = 128
KVH = 8
SHARE = 8
ROWS = 64
REACH = 8
LOG2E = 1.4426950408889634
VMEM_LIMIT = 40 * 1024 * 1024


def doc_starts(lens_ref, token):
    start = jnp.zeros(token.shape, jnp.int32)
    end = jnp.int32(0)
    for d in range(lens_ref.shape[1]):
        length = lens_ref[0, d]
        end = end + length
        start = start + jnp.where(end <= token, length, 0)
    return start


def inverse_frequency(pair):
    return jnp.exp(pair.astype(jnp.float32) * (-2.0 * math.log(ROPE_BASE) / HD))


def key_kernel(
    where_ref, lens_ref, key_hbm, value_hbm, gain_hbm, kv_ref, key_ref, value_ref, gain_ref, sems
):
    copies = [
        pltpu.make_async_copy(key_hbm.at[0], key_ref, sems.at[0]),
        pltpu.make_async_copy(gain_hbm, gain_ref, sems.at[1]),
        pltpu.make_async_copy(value_hbm.at[0], value_ref, sems.at[2]),
    ]
    for copy in copies:
        copy.start()
    token = where_ref[0] * ROWS + lax.broadcasted_iota(jnp.int32, (ROWS, HD), 0)
    lane = lax.broadcasted_iota(jnp.int32, (ROWS, HD), 1)
    position = token - doc_starts(lens_ref, token)
    half = HD // 2
    angles = position.astype(jnp.float32) * inverse_frequency(
        jnp.where(lane < half, lane, lane - half)
    )
    cosine = jnp.cos(angles)
    sine = jnp.sin(angles)
    sine = jnp.where(lane < half, -sine, sine)
    copies[0].wait()
    copies[1].wait()
    gain = gain_ref[...]
    for h in range(KVH):
        values_f = key_ref[:, pl.ds(h * HD, HD)].astype(jnp.float32)
        inv_rms = lax.rsqrt(jnp.mean(values_f * values_f, axis=-1, keepdims=True) + NORM_EPS)
        normed = values_f * inv_rms * gain
        swapped = pltpu.roll(normed, half, 1)
        kv_ref[h, :, :HD] = (normed * cosine + swapped * sine).astype(jnp.bfloat16)
    copies[2].wait()
    for h in range(KVH):
        kv_ref[h, :, HD:] = value_ref[:, pl.ds(h * HD, HD)]


SMEM_SPEC = pl.BlockSpec(memory_space=pltpu.SMEM)
VMEM_SPEC = pl.BlockSpec(memory_space=pltpu.VMEM)
HBM_SPEC = pl.BlockSpec(memory_space=pltpu.HBM)
PARAMS = pltpu.CompilerParams(vmem_limit_bytes=VMEM_LIMIT)


def stay(array):
    return pltpu.with_memory_space_constraint(array, pltpu.HBM)


def prepare_keys(where, lens, key, value, gain):
    return pl.pallas_call(
        key_kernel,
        out_shape=jax.ShapeDtypeStruct((KVH, ROWS, 2 * HD), jnp.bfloat16),
        in_specs=[SMEM_SPEC, SMEM_SPEC, HBM_SPEC, HBM_SPEC, HBM_SPEC],
        out_specs=VMEM_SPEC,
        scratch_shapes=[
            pltpu.VMEM((ROWS, KVH * HD), jnp.bfloat16),
            pltpu.VMEM((ROWS, KVH * HD), jnp.bfloat16),
            pltpu.VMEM((1, HD), jnp.float32),
            pltpu.SemaphoreType.DMA((3,)),
        ],
        compiler_params=PARAMS,
        name="prepare_keys",
    )(where, lens, stay(key), stay(value), stay(gain))


def query_kernel(where_ref, lens_ref, query_hbm, gain_ref, out_ref, query_ref, sems):
    def copy_of(h):
        piece = pl.ds(h * SHARE * HD, SHARE * HD)
        return pltpu.make_async_copy(
            query_hbm.at[0, :, piece], query_ref.at[:, piece], sems.at[h]
        )

    for h in range(KVH):
        copy_of(h).start()
    half = HD // 2
    lane = lax.broadcasted_iota(jnp.int32, (half, 2 * ROWS), 1)
    token = where_ref[0] * ROWS + jnp.where(lane < ROWS, lane, lane - ROWS)
    position = token - doc_starts(lens_ref, token)
    pair = lax.broadcasted_iota(jnp.int32, (half, 2 * ROWS), 0)
    angles = position.astype(jnp.float32) * inverse_frequency(pair)
    cosine = jnp.cos(angles)
    sine = jnp.sin(angles)
    gain = jnp.broadcast_to(gain_ref[...], (HD, HD)).T
    for h in range(KVH):
        copy_of(h).wait()
        for c in range(SHARE // 2):
            column = (h * SHARE + 2 * c) * HD
            both = jnp.concatenate(
                [query_ref[:, pl.ds(column, HD)], query_ref[:, pl.ds(column + HD, HD)]], axis=0
            )
            values_f = both.T.astype(jnp.float32)
            inv_rms = lax.rsqrt(jnp.mean(values_f * values_f, axis=0, keepdims=True) + NORM_EPS)
            normed = values_f * inv_rms * gain
            front, back = normed[:half], normed[half:]
            lanes = pl.ds(c * 2 * ROWS, 2 * ROWS)
            out_ref[h, :half, lanes] = (front * cosine - back * sine).astype(jnp.bfloat16)
            out_ref[h, half:, lanes] = (back * cosine + front * sine).astype(jnp.bfloat16)


def prepare_queries(where, lens, query, gain):
    return pl.pallas_call(
        query_kernel,
        out_shape=jax.ShapeDtypeStruct((KVH, HD, SHARE * ROWS), jnp.bfloat16),
        in_specs=[SMEM_SPEC, SMEM_SPEC, HBM_SPEC, VMEM_SPEC],
        out_specs=VMEM_SPEC,
        scratch_shapes=[
            pltpu.VMEM((ROWS, KVH * SHARE * HD), jnp.bfloat16),
            pltpu.SemaphoreType.DMA((KVH,)),
        ],
        compiler_params=PARAMS,
        cost_estimate=pl.CostEstimate(flops=10_000_000, bytes_accessed=4 << 20, transcendentals=0),
        name="prepare_queries",
    )(where, lens, stay(query), gain)


def visible_bias(where_ref, lens_ref, offsets):
    shape = (ROWS, 2 * ROWS)
    block = where_ref[0]
    lane = lax.broadcasted_iota(jnp.int32, shape, 1)
    token = block * ROWS + jnp.where(lane < ROWS, lane, lane - ROWS)
    start = doc_starts(lens_ref, token)
    row = lax.broadcasted_iota(jnp.int32, shape, 0)
    pieces = []
    for offset in offsets:
        source = (block - offset) * ROWS + row
        seen = (source >= start) & (source <= token)
        pieces.append(jnp.where(seen, 0.0, MASKED))
    return jnp.concatenate(pieces, axis=0)


def masked_scores(h, query_ref, blocks, bias):
    keys = jnp.concatenate([b[h, :, :HD] for b in blocks], axis=0)
    scores = jnp.dot(keys, query_ref[h], preferred_element_type=jnp.float32)
    return scores * (LOG2E / math.sqrt(HD)) + jnp.concatenate([bias] * (SHARE // 2), axis=1)


def mix_values(h, blocks, weights):
    values = jnp.concatenate([b[h, :, HD:] for b in blocks], axis=0)
    return lax.dot_general(
        values,
        weights.astype(jnp.bfloat16),
        (((0,), (0,)), ((), ())),
        preferred_element_type=jnp.float32,
    )


def early_kernel(offsets, where_ref, lens_ref, query_ref, *refs):
    blocks, (acc_ref, stat_ref) = refs[: len(offsets)], refs[len(offsets) :]
    bias = visible_bias(where_ref, lens_ref, offsets)
    for h in range(KVH):
        scores = masked_scores(h, query_ref, blocks, bias)
        top = jnp.max(scores, axis=0, keepdims=True)
        weights = jnp.exp2(scores - top)
        stat_ref[h, 0:1, :] = top
        stat_ref[h, 1:2, :] = jnp.sum(weights, axis=0, keepdims=True)
        acc_ref[h] = mix_values(h, blocks, weights)


def late_kernel(offsets, where_ref, lens_ref, query_ref, acc_ref, stat_ref, *refs):
    blocks, (out_hbm, out_ref, sems) = refs[: len(offsets)], refs[len(offsets) :]
    bias = visible_bias(where_ref, lens_ref, offsets)
    copies = []
    for h in range(KVH):
        scores = masked_scores(h, query_ref, blocks, bias)
        old_top = stat_ref[h, 0:1, :]
        top = jnp.maximum(old_top, jnp.max(scores, axis=0, keepdims=True))
        keep = jnp.exp2(old_top - top)
        weights = jnp.exp2(scores - top)
        denom = stat_ref[h, 1:2, :] * keep + jnp.sum(weights, axis=0, keepdims=True)
        mixed = (acc_ref[h] * keep + mix_values(h, blocks, weights)) / denom
        rounded = mixed.astype(jnp.bfloat16)
        for c in range(SHARE // 2):
            both = rounded[:, c * 2 * ROWS : (c + 1) * 2 * ROWS].T
            column = (h * SHARE + 2 * c) * HD
            out_ref[:, pl.ds(column, HD)] = both[:ROWS]
            out_ref[:, pl.ds(column + HD, HD)] = both[ROWS:]
        piece = pl.ds(h * SHARE * HD, SHARE * HD)
        copies.append(
            pltpu.make_async_copy(out_ref.at[:, piece], out_hbm.at[0, :, piece], sems.at[h])
        )
        copies[-1].start()
    for copy in copies:
        copy.wait()


def attention_cost(count):
    return pl.CostEstimate(
        flops=4 * KVH * SHARE * ROWS * ROWS * HD * count,
        bytes_accessed=4 << 20,
        transcendentals=KVH * SHARE * ROWS * ROWS * count,
    )


def attend_early(offsets, where, lens, query, blocks):
    count = len(offsets)
    return pl.pallas_call(
        lambda *refs: early_kernel(offsets, *refs),
        out_shape=(
            jax.ShapeDtypeStruct((KVH, HD, SHARE * ROWS), jnp.float32),
            jax.ShapeDtypeStruct((KVH, 8, SHARE * ROWS), jnp.float32),
        ),
        in_specs=[SMEM_SPEC, SMEM_SPEC] + [VMEM_SPEC] * (1 + count),
        out_specs=(VMEM_SPEC, VMEM_SPEC),
        compiler_params=PARAMS,
        cost_estimate=attention_cost(count),
        name="attend_early",
    )(where, lens, query, *blocks)


def attend_late(offsets, where, lens, query, acc, stat, blocks):
    count = len(offsets)
    return pl.pallas_call(
        lambda *refs: late_kernel(offsets, *refs),
        out_shape=jax.ShapeDtypeStruct((1, ROWS, KVH * SHARE * HD), jnp.bfloat16),
        in_specs=[SMEM_SPEC, SMEM_SPEC] + [VMEM_SPEC] * (3 + count),
        out_specs=HBM_SPEC,
        scratch_shapes=[
            pltpu.VMEM((ROWS, KVH * SHARE * HD), jnp.bfloat16),
            pltpu.SemaphoreType.DMA((KVH,)),
        ],
        compiler_params=PARAMS,
        cost_estimate=attention_cost(count),
        name="attend_late",
    )(where, lens, query, acc, stat, *blocks)


def plus_pairs(count, step):
    return [(i, i + 1) for i in range(count - 1) if i + 1 >= step]


def cross_pairs(count):
    return [(i, i + REACH) for i in range(REACH)] + [(REACH + i, i) for i in range(3)]


def minus_pairs(count, step):
    receivers = list(range(REACH - step, count)) + list(range(0, 3 - step))
    return [((r + 1) % count, r) for r in receivers]


def slot_pairs(seqs, groups):
    pairs = []
    spread = groups // KVH
    for s in range(seqs):
        repeat, place = divmod(s, KVH)
        for g in range(groups):
            head, page = divmod(g, spread)
            entry = head * 2 + repeat
            pairs.append((s * groups + g, entry * groups + place * spread + page))
    return pairs


def body(query_proj, key_proj, value_proj, query_gain, key_gain, doc_lengths):
    seqs = lax.axis_size("seq")
    groups = lax.axis_size("group")
    where = lax.axis_index("seq").astype(jnp.int32).reshape(1)
    kv = prepare_keys(where, doc_lengths, key_proj, value_proj, key_gain.reshape(1, HD))
    plus = [lax.ppermute(kv, "seq", plus_pairs(seqs, 1))]
    minus = [lax.ppermute(kv, "seq", cross_pairs(seqs))]
    for step in (2, 3, 4):
        plus.append(lax.ppermute(plus[-1], "seq", plus_pairs(seqs, step)))
        minus.append(lax.ppermute(minus[-1], "seq", minus_pairs(seqs, step - 1)))
    query = prepare_queries(where, doc_lengths, query_proj, query_gain.reshape(1, HD))
    pages = kv.reshape(KVH * (ROWS // PAGE), PAGE, 2 * HD)
    mine = lax.all_to_all(pages, "group", split_axis=0, concat_axis=0, tiled=True)
    cache = lax.ppermute(mine, ("seq", "group"), slot_pairs(seqs, groups))
    acc, stat = attend_early(
        (0, 1, 2, 3, 8, 7, 6), where, doc_lengths, query, [kv] + plus[:3] + minus[:3]
    )
    attended = attend_late((4, 5), where, doc_lengths, query, acc, stat, [plus[3], minus[3]])
    return attended, cache.reshape(1, 1, groups, 1, PAGE, 2 * HD)


def solution(mesh):
    in_specs = (
        P("group", "seq", None),
        P("group", "seq", None),
        P("group", "seq", None),
        P(),
        P(),
        P("group", None),
    )
    out_specs = (P("seq", "group", None, None, None, None),)
    out_specs = (P("group", "seq", None),) + out_specs
    return jax.shard_map(body, mesh=mesh, in_specs=in_specs, out_specs=out_specs, check_vma=False)
```

```python
import math

import jax
import jax.numpy as jnp
from jax import lax
from jax.experimental import pallas as pl
from jax.experimental.pallas import tpu as pltpu
from jax.sharding import PartitionSpec as P

PAGE = 16
NORM_EPS = 1e-06
ROPE_BASE = 1000000.0
MASKED = -1e30
HD = 128
KVH = 8
SHARE = 8
ROWS = 64
REACH = 8
LOG2E = 1.4426950408889634
VMEM_LIMIT = 20 * 1024 * 1024


def doc_starts(lens_ref, token):
    start = jnp.zeros(token.shape, jnp.int32)
    end = jnp.int32(0)
    for d in range(lens_ref.shape[1]):
        length = lens_ref[0, d]
        end = end + length
        start = start + jnp.where(end <= token, length, 0)
    return start


def inverse_frequency(pair):
    return jnp.exp(pair.astype(jnp.float32) * (-2.0 * math.log(ROPE_BASE) / HD))


def key_kernel(
    where_ref, lens_ref, key_hbm, value_hbm, gain_hbm, kv_ref, key_ref, value_ref, gain_ref, sems
):
    copies = [
        pltpu.make_async_copy(key_hbm.at[0], key_ref, sems.at[0]),
        pltpu.make_async_copy(gain_hbm, gain_ref, sems.at[1]),
        pltpu.make_async_copy(value_hbm.at[0], value_ref, sems.at[2]),
    ]
    for copy in copies:
        copy.start()
    token = where_ref[0] * ROWS + lax.broadcasted_iota(jnp.int32, (ROWS, HD), 0)
    lane = lax.broadcasted_iota(jnp.int32, (ROWS, HD), 1)
    position = token - doc_starts(lens_ref, token)
    half = HD // 2
    angles = position.astype(jnp.float32) * inverse_frequency(
        jnp.where(lane < half, lane, lane - half)
    )
    cosine = jnp.cos(angles)
    sine = jnp.sin(angles)
    sine = jnp.where(lane < half, -sine, sine)
    copies[0].wait()
    copies[1].wait()
    gain = gain_ref[...]
    for h in range(KVH):
        values_f = key_ref[:, pl.ds(h * HD, HD)].astype(jnp.float32)
        inv_rms = lax.rsqrt(jnp.mean(values_f * values_f, axis=-1, keepdims=True) + NORM_EPS)
        normed = values_f * inv_rms * gain
        swapped = pltpu.roll(normed, half, 1)
        kv_ref[h, :, :HD] = (normed * cosine + swapped * sine).astype(jnp.bfloat16)
    copies[2].wait()
    for h in range(KVH):
        kv_ref[h, :, HD:] = value_ref[:, pl.ds(h * HD, HD)]


SMEM_SPEC = pl.BlockSpec(memory_space=pltpu.SMEM)
VMEM_SPEC = pl.BlockSpec(memory_space=pltpu.VMEM)
HBM_SPEC = pl.BlockSpec(memory_space=pltpu.HBM)
PARAMS = pltpu.CompilerParams(vmem_limit_bytes=VMEM_LIMIT)


def stay(array):
    return pltpu.with_memory_space_constraint(array, pltpu.HBM)


def prepare_keys(where, lens, key, value, gain):
    return pl.pallas_call(
        key_kernel,
        out_shape=jax.ShapeDtypeStruct((KVH, ROWS, 2 * HD), jnp.bfloat16),
        in_specs=[SMEM_SPEC, SMEM_SPEC, HBM_SPEC, HBM_SPEC, HBM_SPEC],
        out_specs=VMEM_SPEC,
        scratch_shapes=[
            pltpu.VMEM((ROWS, KVH * HD), jnp.bfloat16),
            pltpu.VMEM((ROWS, KVH * HD), jnp.bfloat16),
            pltpu.VMEM((1, HD), jnp.float32),
            pltpu.SemaphoreType.DMA((3,)),
        ],
        compiler_params=PARAMS,
        name="prepare_keys",
    )(where, stay(lens), stay(key), stay(value), stay(gain))


def query_kernel(where_ref, lens_ref, query_hbm, gain_ref, out_ref, query_ref, sems):
    def copy_of(h):
        piece = pl.ds(h * SHARE * HD, SHARE * HD)
        return pltpu.make_async_copy(
            query_hbm.at[0, :, piece], query_ref.at[:, piece], sems.at[h]
        )

    for h in range(KVH):
        copy_of(h).start()
    half = HD // 2
    lane = lax.broadcasted_iota(jnp.int32, (half, 2 * ROWS), 1)
    token = where_ref[0] * ROWS + jnp.where(lane < ROWS, lane, lane - ROWS)
    position = token - doc_starts(lens_ref, token)
    pair = lax.broadcasted_iota(jnp.int32, (half, 2 * ROWS), 0)
    angles = position.astype(jnp.float32) * inverse_frequency(pair)
    cosine = jnp.cos(angles)
    sine = jnp.sin(angles)
    gain = jnp.broadcast_to(gain_ref[...], (HD, HD)).T
    for h in range(KVH):
        copy_of(h).wait()
        for c in range(SHARE // 2):
            column = (h * SHARE + 2 * c) * HD
            both = jnp.concatenate(
                [query_ref[:, pl.ds(column, HD)], query_ref[:, pl.ds(column + HD, HD)]], axis=0
            )
            values_f = both.T.astype(jnp.float32)
            inv_rms = lax.rsqrt(jnp.mean(values_f * values_f, axis=0, keepdims=True) + NORM_EPS)
            normed = values_f * inv_rms * gain
            front, back = normed[:half], normed[half:]
            lanes = pl.ds(c * 2 * ROWS, 2 * ROWS)
            out_ref[h, :half, lanes] = (front * cosine - back * sine).astype(jnp.bfloat16)
            out_ref[h, half:, lanes] = (back * cosine + front * sine).astype(jnp.bfloat16)


def prepare_queries(where, lens, query, gain):
    return pl.pallas_call(
        query_kernel,
        out_shape=jax.ShapeDtypeStruct((KVH, HD, SHARE * ROWS), jnp.bfloat16),
        in_specs=[SMEM_SPEC, SMEM_SPEC, HBM_SPEC, VMEM_SPEC],
        out_specs=VMEM_SPEC,
        scratch_shapes=[
            pltpu.VMEM((ROWS, KVH * SHARE * HD), jnp.bfloat16),
            pltpu.SemaphoreType.DMA((KVH,)),
        ],
        compiler_params=PARAMS,
        cost_estimate=pl.CostEstimate(flops=10_000_000, bytes_accessed=4 << 20, transcendentals=0),
        name="prepare_queries",
    )(where, stay(lens), stay(query), stay(gain))


def visible_bias(where_ref, lens_ref, offsets):
    shape = (ROWS, 2 * ROWS)
    block = where_ref[0]
    lane = lax.broadcasted_iota(jnp.int32, shape, 1)
    token = block * ROWS + jnp.where(lane < ROWS, lane, lane - ROWS)
    start = doc_starts(lens_ref, token)
    row = lax.broadcasted_iota(jnp.int32, shape, 0)
    pieces = []
    for offset in offsets:
        source = (block - offset) * ROWS + row
        seen = (source >= start) & (source <= token)
        pieces.append(jnp.where(seen, 0.0, MASKED))
    return jnp.concatenate(pieces, axis=0)


def masked_scores(h, query_ref, blocks, bias):
    keys = jnp.concatenate([b[h, :, :HD] for b in blocks], axis=0)
    scores = jnp.dot(keys, query_ref[h], preferred_element_type=jnp.float32)
    return scores * (LOG2E / math.sqrt(HD)) + jnp.concatenate([bias] * (SHARE // 2), axis=1)


def mix_values(h, blocks, weights):
    values = jnp.concatenate([b[h, :, HD:] for b in blocks], axis=0)
    return lax.dot_general(
        values,
        weights.astype(jnp.bfloat16),
        (((0,), (0,)), ((), ())),
        preferred_element_type=jnp.float32,
    )


def early_kernel(offsets, where_ref, lens_ref, query_ref, *refs):
    blocks, (acc_ref, stat_ref) = refs[: len(offsets)], refs[len(offsets) :]
    bias = visible_bias(where_ref, lens_ref, offsets)
    for h in range(KVH):
        scores = masked_scores(h, query_ref, blocks, bias)
        top = jnp.max(scores, axis=0, keepdims=True)
        weights = jnp.exp2(scores - top)
        stat_ref[h, 0:1, :] = top
        stat_ref[h, 1:2, :] = jnp.sum(weights, axis=0, keepdims=True)
        acc_ref[h] = mix_values(h, blocks, weights)


def late_kernel(offsets, where_ref, lens_ref, query_ref, acc_ref, stat_ref, *refs):
    blocks, (out_hbm, out_ref, sems) = refs[: len(offsets)], refs[len(offsets) :]
    bias = visible_bias(where_ref, lens_ref, offsets)
    copies = []
    for h in range(KVH):
        scores = masked_scores(h, query_ref, blocks, bias)
        old_top = stat_ref[h, 0:1, :]
        top = jnp.maximum(old_top, jnp.max(scores, axis=0, keepdims=True))
        keep = jnp.exp2(old_top - top)
        weights = jnp.exp2(scores - top)
        denom = stat_ref[h, 1:2, :] * keep + jnp.sum(weights, axis=0, keepdims=True)
        mixed = acc_ref[h] * keep + mix_values(h, blocks, weights)
        rounded = (mixed * (1.0 / denom)).astype(jnp.bfloat16)
        for c in range(SHARE // 2):
            both = rounded[:, c * 2 * ROWS : (c + 1) * 2 * ROWS].T
            column = (h * SHARE + 2 * c) * HD
            out_ref[:, pl.ds(column, HD)] = both[:ROWS]
            out_ref[:, pl.ds(column + HD, HD)] = both[ROWS:]
        piece = pl.ds(h * SHARE * HD, SHARE * HD)
        copies.append(
            pltpu.make_async_copy(out_ref.at[:, piece], out_hbm.at[0, :, piece], sems.at[h])
        )
        copies[-1].start()
    for copy in copies:
        copy.wait()


def attention_cost(count):
    return pl.CostEstimate(
        flops=4 * KVH * SHARE * ROWS * ROWS * HD * count,
        bytes_accessed=4 << 20,
        transcendentals=KVH * SHARE * ROWS * ROWS * count,
    )


def attend_early(offsets, where, lens, query, blocks):
    count = len(offsets)
    return pl.pallas_call(
        lambda *refs: early_kernel(offsets, *refs),
        out_shape=(
            jax.ShapeDtypeStruct((KVH, HD, SHARE * ROWS), jnp.float32),
            jax.ShapeDtypeStruct((KVH, 8, SHARE * ROWS), jnp.float32),
        ),
        in_specs=[SMEM_SPEC, SMEM_SPEC] + [VMEM_SPEC] * (1 + count),
        out_specs=(VMEM_SPEC, VMEM_SPEC),
        compiler_params=PARAMS,
        cost_estimate=attention_cost(count),
        name="attend_early",
    )(where, stay(lens), query, *blocks)


def attend_late(offsets, where, lens, query, acc, stat, blocks):
    count = len(offsets)
    return pl.pallas_call(
        lambda *refs: late_kernel(offsets, *refs),
        out_shape=jax.ShapeDtypeStruct((1, ROWS, KVH * SHARE * HD), jnp.bfloat16),
        in_specs=[SMEM_SPEC, SMEM_SPEC] + [VMEM_SPEC] * (3 + count),
        out_specs=HBM_SPEC,
        scratch_shapes=[
            pltpu.VMEM((ROWS, KVH * SHARE * HD), jnp.bfloat16),
            pltpu.SemaphoreType.DMA((KVH,)),
        ],
        compiler_params=PARAMS,
        cost_estimate=attention_cost(count),
        name="attend_late",
    )(where, stay(lens), query, acc, stat, *blocks)


def pages_kernel(where_ref, kv_ref, out_ref):
    place = jnp.bitwise_and(where_ref[0], KVH - 1)
    for h in range(KVH):
        out_ref[h] = kv_ref[jnp.bitwise_xor(place, h)]


def order_pages(where, kv):
    return pl.pallas_call(
        pages_kernel,
        out_shape=jax.ShapeDtypeStruct((KVH, ROWS, 2 * HD), jnp.bfloat16),
        in_specs=[SMEM_SPEC, VMEM_SPEC],
        out_specs=VMEM_SPEC,
        compiler_params=PARAMS,
        name="order_pages",
    )(where, kv)


def plus_pairs(count, step):
    return [(i, i + 1) for i in range(count - 1) if i + 1 >= step]


def cross_pairs(count):
    return [(i, i + REACH) for i in range(REACH)] + [(REACH + i, i) for i in range(3)]


def minus_pairs(count, step):
    receivers = list(range(REACH - step, count)) + list(range(0, 3 - step))
    return [((r + 1) % count, r) for r in receivers]


def slot_pairs(seqs, groups):
    pairs = []
    spread = groups // KVH
    for s in range(seqs):
        repeat, place = divmod(s, KVH)
        for g in range(groups):
            slot, page = divmod(g, spread)
            entry = (slot ^ place) * 2 + repeat
            pairs.append((s * groups + g, entry * groups + place * spread + page))
    return pairs


def body(query_proj, key_proj, value_proj, query_gain, key_gain, doc_lengths):
    seqs = lax.axis_size("seq")
    groups = lax.axis_size("group")
    where = lax.axis_index("seq").astype(jnp.int32).reshape(1)
    kv = prepare_keys(where, doc_lengths, key_proj, value_proj, key_gain.reshape(1, HD))
    minus8 = lax.ppermute(kv, "seq", cross_pairs(seqs))
    minus1 = lax.ppermute(kv, "seq", plus_pairs(seqs, 1))
    pages = order_pages(where, kv).reshape(groups, PAGE, 2 * HD)
    mine = lax.all_to_all(pages, "group", split_axis=0, concat_axis=0, tiled=True)
    minus8, minus1, later = lax.optimization_barrier((minus8, minus1, where))
    minus7 = lax.ppermute(minus8, "seq", minus_pairs(seqs, 1))
    minus2 = lax.ppermute(minus1, "seq", plus_pairs(seqs, 2))
    query = prepare_queries(later, doc_lengths, query_proj, query_gain.reshape(1, HD))
    minus7, minus2, query, mine = lax.optimization_barrier((minus7, minus2, query, mine))
    minus6 = lax.ppermute(minus7, "seq", minus_pairs(seqs, 2))
    minus3 = lax.ppermute(minus2, "seq", plus_pairs(seqs, 3))
    cache = lax.ppermute(mine, ("seq", "group"), slot_pairs(seqs, groups))
    minus6, minus3 = lax.optimization_barrier((minus6, minus3))
    minus5 = lax.ppermute(minus6, "seq", minus_pairs(seqs, 3))
    minus4 = lax.ppermute(minus3, "seq", plus_pairs(seqs, 4))
    acc, stat = attend_early(
        (0, 1, 8, 2, 7, 3, 6),
        where,
        doc_lengths,
        query,
        [kv, minus1, minus8, minus2, minus7, minus3, minus6],
    )
    attended = attend_late((4, 5), where, doc_lengths, query, acc, stat, [minus4, minus5])
    return attended, cache.reshape(1, 1, groups, 1, PAGE, 2 * HD)


def solution(mesh):
    rows = P("group", "seq", None)
    in_specs = (rows, rows, rows, P(), P(), P("group", None))
    out_specs = (rows, P("seq", "group", None, None, None, None))
    return jax.shard_map(body, mesh=mesh, in_specs=in_specs, out_specs=out_specs, check_vma=False)
```

```python
import math

import jax
import jax.numpy as jnp
from jax import lax
from jax.experimental import pallas as pl
from jax.experimental.pallas import tpu as pltpu
from jax.sharding import PartitionSpec as P

PAGE = 16
NORM_EPS = 1e-06
ROPE_BASE = 1000000.0
MASKED = -1e30
HD = 128
KVH = 8
SHARE = 8
ROWS = 64
REACH = 8
LOG2E = 1.4426950408889634
VMEM_LIMIT = 20 * 1024 * 1024


def doc_starts(lens_ref, token):
    start = jnp.zeros(token.shape, jnp.int32)
    end = jnp.int32(0)
    for d in range(lens_ref.shape[1]):
        length = lens_ref[0, d]
        end = end + length
        start = start + jnp.where(end <= token, length, 0)
    return start


def inverse_frequency(pair):
    return jnp.exp(pair.astype(jnp.float32) * (-2.0 * math.log(ROPE_BASE) / HD))


def key_kernel(
    where_ref, lens_ref, key_hbm, value_hbm, gain_hbm, kv_ref, key_ref, value_ref, gain_ref, sems
):
    copies = [
        pltpu.make_async_copy(key_hbm.at[0], key_ref, sems.at[0]),
        pltpu.make_async_copy(gain_hbm, gain_ref, sems.at[1]),
        pltpu.make_async_copy(value_hbm.at[0], value_ref, sems.at[2]),
    ]
    for copy in copies:
        copy.start()
    token = where_ref[0] * ROWS + lax.broadcasted_iota(jnp.int32, (ROWS, HD), 0)
    lane = lax.broadcasted_iota(jnp.int32, (ROWS, HD), 1)
    position = token - doc_starts(lens_ref, token)
    half = HD // 2
    angles = position.astype(jnp.float32) * inverse_frequency(
        jnp.where(lane < half, lane, lane - half)
    )
    cosine = jnp.cos(angles)
    sine = jnp.sin(angles)
    sine = jnp.where(lane < half, -sine, sine)
    copies[0].wait()
    copies[1].wait()
    gain = gain_ref[...]
    for h in range(KVH):
        values_f = key_ref[:, pl.ds(h * HD, HD)].astype(jnp.float32)
        inv_rms = lax.rsqrt(jnp.mean(values_f * values_f, axis=-1, keepdims=True) + NORM_EPS)
        normed = values_f * inv_rms * gain
        swapped = pltpu.roll(normed, half, 1)
        kv_ref[h, :, :HD] = (normed * cosine + swapped * sine).astype(jnp.bfloat16)
    copies[2].wait()
    for h in range(KVH):
        kv_ref[h, :, HD:] = value_ref[:, pl.ds(h * HD, HD)]


SMEM_SPEC = pl.BlockSpec(memory_space=pltpu.SMEM)
VMEM_SPEC = pl.BlockSpec(memory_space=pltpu.VMEM)
HBM_SPEC = pl.BlockSpec(memory_space=pltpu.HBM)
PARAMS = pltpu.CompilerParams(vmem_limit_bytes=VMEM_LIMIT)


def stay(array):
    return pltpu.with_memory_space_constraint(array, pltpu.HBM)


def prepare_keys(where, lens, key, value, gain):
    return pl.pallas_call(
        key_kernel,
        out_shape=jax.ShapeDtypeStruct((KVH, ROWS, 2 * HD), jnp.bfloat16),
        in_specs=[SMEM_SPEC, SMEM_SPEC, HBM_SPEC, HBM_SPEC, HBM_SPEC],
        out_specs=VMEM_SPEC,
        scratch_shapes=[
            pltpu.VMEM((ROWS, KVH * HD), jnp.bfloat16),
            pltpu.VMEM((ROWS, KVH * HD), jnp.bfloat16),
            pltpu.VMEM((1, HD), jnp.float32),
            pltpu.SemaphoreType.DMA((3,)),
        ],
        compiler_params=PARAMS,
        name="prepare_keys",
    )(where, stay(lens), stay(key), stay(value), stay(gain))


def query_kernel(where_ref, lens_ref, query_hbm, gain_ref, out_ref, query_ref, sems):
    def copy_of(h):
        piece = pl.ds(h * SHARE * HD, SHARE * HD)
        return pltpu.make_async_copy(
            query_hbm.at[0, :, piece], query_ref.at[:, piece], sems.at[h]
        )

    for h in range(KVH):
        copy_of(h).start()
    half = HD // 2
    lane = lax.broadcasted_iota(jnp.int32, (half, 2 * ROWS), 1)
    token = where_ref[0] * ROWS + jnp.where(lane < ROWS, lane, lane - ROWS)
    position = token - doc_starts(lens_ref, token)
    pair = lax.broadcasted_iota(jnp.int32, (half, 2 * ROWS), 0)
    angles = position.astype(jnp.float32) * inverse_frequency(pair)
    cosine = jnp.cos(angles)
    sine = jnp.sin(angles)
    gain = jnp.broadcast_to(gain_ref[...], (HD, HD)).T
    for h in range(KVH):
        copy_of(h).wait()
        for c in range(SHARE // 2):
            column = (h * SHARE + 2 * c) * HD
            both = jnp.concatenate(
                [query_ref[:, pl.ds(column, HD)], query_ref[:, pl.ds(column + HD, HD)]], axis=0
            )
            values_f = both.T.astype(jnp.float32)
            inv_rms = lax.rsqrt(jnp.mean(values_f * values_f, axis=0, keepdims=True) + NORM_EPS)
            normed = values_f * inv_rms * gain
            front, back = normed[:half], normed[half:]
            lanes = pl.ds(c * 2 * ROWS, 2 * ROWS)
            out_ref[h, :half, lanes] = (front * cosine - back * sine).astype(jnp.bfloat16)
            out_ref[h, half:, lanes] = (back * cosine + front * sine).astype(jnp.bfloat16)


def prepare_queries(where, lens, query, gain):
    return pl.pallas_call(
        query_kernel,
        out_shape=jax.ShapeDtypeStruct((KVH, HD, SHARE * ROWS), jnp.bfloat16),
        in_specs=[SMEM_SPEC, SMEM_SPEC, HBM_SPEC, VMEM_SPEC],
        out_specs=VMEM_SPEC,
        scratch_shapes=[
            pltpu.VMEM((ROWS, KVH * SHARE * HD), jnp.bfloat16),
            pltpu.SemaphoreType.DMA((KVH,)),
        ],
        compiler_params=PARAMS,
        cost_estimate=pl.CostEstimate(flops=10_000_000, bytes_accessed=4 << 20, transcendentals=0),
        name="prepare_queries",
    )(where, stay(lens), stay(query), stay(gain))


def visible_bias(where_ref, lens_ref, offsets):
    shape = (ROWS, 2 * ROWS)
    block = where_ref[0]
    lane = lax.broadcasted_iota(jnp.int32, shape, 1)
    token = block * ROWS + jnp.where(lane < ROWS, lane, lane - ROWS)
    start = doc_starts(lens_ref, token)
    row = lax.broadcasted_iota(jnp.int32, shape, 0)
    pieces = []
    for offset in offsets:
        source = (block - offset) * ROWS + row
        seen = (source >= start) & (source <= token)
        pieces.append(jnp.where(seen, 0.0, MASKED))
    return jnp.concatenate(pieces, axis=0)


def masked_scores(h, query_ref, parts, bias):
    keys = jnp.concatenate([p[:, :HD] for p in parts], axis=0)
    scores = jnp.dot(keys, query_ref[h], preferred_element_type=jnp.float32)
    return scores * (LOG2E / math.sqrt(HD)) + jnp.concatenate([bias] * (SHARE // 2), axis=1)


def mix_values(parts, weights):
    values = jnp.concatenate([p[:, HD:] for p in parts], axis=0)
    return lax.dot_general(
        values,
        weights.astype(jnp.bfloat16),
        (((0,), (0,)), ((), ())),
        preferred_element_type=jnp.float32,
    )


def early_kernel(offsets, where_ref, lens_ref, query_ref, *refs):
    blocks, (acc_ref, stat_ref) = refs[: len(offsets)], refs[len(offsets) :]
    bias = visible_bias(where_ref, lens_ref, offsets)
    for h in range(KVH):
        parts = [b[h] for b in blocks]
        scores = masked_scores(h, query_ref, parts, bias)
        top = jnp.max(scores, axis=0, keepdims=True)
        weights = jnp.exp2(scores - top)
        stat_ref[h, 0:1, :] = top
        stat_ref[h, 1:2, :] = jnp.sum(weights, axis=0, keepdims=True)
        acc_ref[h] = mix_values(parts, weights)


def late_kernel(offsets, where_ref, lens_ref, query_ref, acc_ref, stat_ref, *refs):
    count = len(offsets)
    blocks, other_ref, (out_hbm, out_ref, sems) = refs[:count], refs[count], refs[count + 1 :]
    bias = visible_bias(where_ref, lens_ref, offsets)
    own = where_ref[0]
    use_other = jnp.logical_and(own >= REACH, own < REACH + REACH // 2)
    copies = []
    for h in range(KVH):
        last = jnp.where(use_other, other_ref[h], blocks[-1][h])
        parts = [b[h] for b in blocks[:-1]] + [last]
        scores = masked_scores(h, query_ref, parts, bias)
        old_top = stat_ref[h, 0:1, :]
        top = jnp.maximum(old_top, jnp.max(scores, axis=0, keepdims=True))
        keep = jnp.exp2(old_top - top)
        weights = jnp.exp2(scores - top)
        denom = stat_ref[h, 1:2, :] * keep + jnp.sum(weights, axis=0, keepdims=True)
        mixed = acc_ref[h] * keep + mix_values(parts, weights)
        rounded = (mixed * (1.0 / denom)).astype(jnp.bfloat16)
        for c in range(SHARE // 2):
            both = rounded[:, c * 2 * ROWS : (c + 1) * 2 * ROWS].T
            column = (h * SHARE + 2 * c) * HD
            out_ref[:, pl.ds(column, HD)] = both[:ROWS]
            out_ref[:, pl.ds(column + HD, HD)] = both[ROWS:]
        piece = pl.ds(h * SHARE * HD, SHARE * HD)
        copies.append(
            pltpu.make_async_copy(out_ref.at[:, piece], out_hbm.at[0, :, piece], sems.at[h])
        )
        copies[-1].start()
    for copy in copies:
        copy.wait()


def attention_cost(count):
    return pl.CostEstimate(
        flops=4 * KVH * SHARE * ROWS * ROWS * HD * count,
        bytes_accessed=4 << 20,
        transcendentals=KVH * SHARE * ROWS * ROWS * count,
    )


def attend_early(offsets, where, lens, query, blocks):
    count = len(offsets)
    return pl.pallas_call(
        lambda *refs: early_kernel(offsets, *refs),
        out_shape=(
            jax.ShapeDtypeStruct((KVH, HD, SHARE * ROWS), jnp.float32),
            jax.ShapeDtypeStruct((KVH, 8, SHARE * ROWS), jnp.float32),
        ),
        in_specs=[SMEM_SPEC, SMEM_SPEC] + [VMEM_SPEC] * (1 + count),
        out_specs=(VMEM_SPEC, VMEM_SPEC),
        compiler_params=PARAMS,
        cost_estimate=attention_cost(count),
        name="attend_early",
    )(where, stay(lens), query, *blocks)


def attend_late(offsets, where, lens, query, acc, stat, blocks):
    count = len(offsets)
    return pl.pallas_call(
        lambda *refs: late_kernel(offsets, *refs),
        out_shape=jax.ShapeDtypeStruct((1, ROWS, KVH * SHARE * HD), jnp.bfloat16),
        in_specs=[SMEM_SPEC, SMEM_SPEC] + [VMEM_SPEC] * (3 + count + 1),
        out_specs=HBM_SPEC,
        scratch_shapes=[
            pltpu.VMEM((ROWS, KVH * SHARE * HD), jnp.bfloat16),
            pltpu.SemaphoreType.DMA((KVH,)),
        ],
        compiler_params=PARAMS,
        cost_estimate=attention_cost(count),
        name="attend_late",
    )(where, stay(lens), query, acc, stat, *blocks)


def pages_kernel(where_ref, kv_ref, out_ref):
    place = jnp.bitwise_and(where_ref[0], KVH - 1)
    for h in range(KVH):
        out_ref[h] = kv_ref[jnp.bitwise_xor(place, h)]


def order_pages(where, kv):
    return pl.pallas_call(
        pages_kernel,
        out_shape=jax.ShapeDtypeStruct((KVH, ROWS, 2 * HD), jnp.bfloat16),
        in_specs=[SMEM_SPEC, VMEM_SPEC],
        out_specs=VMEM_SPEC,
        compiler_params=PARAMS,
        name="order_pages",
    )(where, kv)


def plus_pairs(count, step):
    receivers = range(step, count)
    if step == REACH // 2:
        receivers = [r for r in receivers if r % REACH >= step]
    return [(r - 1, r) for r in receivers]


def diagonal_pairs(count):
    return [(i, i + REACH - 1) for i in range(count - REACH + 1)] + [
        (REACH + 1 + i, i) for i in range(2)
    ]


def partner_pairs(count):
    return [(i, i + REACH) for i in range(count - REACH)]


def minus_pairs(count, step):
    if step == REACH // 2:
        return [(r + 1, r) for r in range(REACH, REACH + step)]
    receivers = list(range(REACH - step, count)) + list(range(0, 3 - step))
    return [((r + 1) % count, r) for r in receivers]


def slot_pairs(seqs, groups):
    pairs = []
    spread = groups // KVH
    for s in range(seqs):
        repeat, place = divmod(s, KVH)
        for g in range(groups):
            slot, page = divmod(g, spread)
            entry = (slot ^ place) * 2 + repeat
            pairs.append((s * groups + g, entry * groups + place * spread + page))
    return pairs


def body(query_proj, key_proj, value_proj, query_gain, key_gain, doc_lengths):
    seqs = lax.axis_size("seq")
    groups = lax.axis_size("group")
    where = lax.axis_index("seq").astype(jnp.int32).reshape(1)
    kv = prepare_keys(where, doc_lengths, key_proj, value_proj, key_gain.reshape(1, HD))
    minus1 = lax.ppermute(kv, "seq", plus_pairs(seqs, 1))
    minus7 = lax.ppermute(kv, "seq", diagonal_pairs(seqs))
    minus8 = lax.ppermute(kv, "seq", partner_pairs(seqs))
    pages = order_pages(where, kv).reshape(groups, PAGE, 2 * HD)
    mine = lax.all_to_all(pages, "group", split_axis=0, concat_axis=0, tiled=True)
    minus2 = lax.ppermute(minus1, "seq", plus_pairs(seqs, 2))
    minus6 = lax.ppermute(minus7, "seq", minus_pairs(seqs, 2))
    minus1, later = lax.optimization_barrier((minus1, where))
    query = prepare_queries(later, doc_lengths, query_proj, query_gain.reshape(1, HD))
    minus2, query, mine = lax.optimization_barrier((minus2, query, mine))
    minus3 = lax.ppermute(minus2, "seq", plus_pairs(seqs, 3))
    minus5 = lax.ppermute(minus6, "seq", minus_pairs(seqs, 3))
    cache = lax.ppermute(mine, ("seq", "group"), slot_pairs(seqs, groups))
    acc, stat = attend_early(
        (0, 1, 7, 8, 2, 6), where, doc_lengths, query, [kv, minus1, minus7, minus8, minus2, minus6]
    )
    minus3, acc = lax.optimization_barrier((minus3, acc))
    plus4 = lax.ppermute(minus3, "seq", plus_pairs(seqs, 4))
    minus4 = lax.ppermute(minus5, "seq", minus_pairs(seqs, 4))
    attended = attend_late(
        (3, 5, 4), where, doc_lengths, query, acc, stat, [minus3, minus5, plus4, minus4]
    )
    return attended, cache.reshape(1, 1, groups, 1, PAGE, 2 * HD)


def solution(mesh):
    rows = P("group", "seq", None)
    in_specs = (rows, rows, rows, P(), P(), P("group", None))
    out_specs = (rows, P("seq", "group", None, None, None, None))
    return jax.shard_map(body, mesh=mesh, in_specs=in_specs, out_specs=out_specs, check_vma=False)
```

```python
import math

import jax
import jax.numpy as jnp
from jax import lax
from jax.experimental import pallas as pl
from jax.experimental.pallas import tpu as pltpu
from jax.sharding import PartitionSpec as P

PAGE = 16
NORM_EPS = 1e-06
ROPE_BASE = 1000000.0
MASKED = -1e30
HD = 128
KVH = 8
SHARE = 8
ROWS = 64
REACH = 8
LOG2E = 1.4426950408889634
VMEM_LIMIT = 20 * 1024 * 1024


def doc_starts(lens_ref, token):
    start = jnp.zeros(token.shape, jnp.int32)
    end = jnp.int32(0)
    for d in range(lens_ref.shape[1]):
        length = lens_ref[0, d]
        end = end + length
        start = start + jnp.where(end <= token, length, 0)
    return start


def inverse_frequency(pair):
    return jnp.exp(pair.astype(jnp.float32) * (-2.0 * math.log(ROPE_BASE) / HD))


def key_kernel(
    where_ref, lens_ref, key_hbm, value_hbm, gain_hbm, kv_ref, key_ref, value_ref, gain_ref, sems
):
    copies = [
        pltpu.make_async_copy(key_hbm.at[0], key_ref, sems.at[0]),
        pltpu.make_async_copy(gain_hbm, gain_ref, sems.at[1]),
        pltpu.make_async_copy(value_hbm.at[0], value_ref, sems.at[2]),
    ]
    for copy in copies:
        copy.start()
    token = where_ref[0] * ROWS + lax.broadcasted_iota(jnp.int32, (ROWS, HD), 0)
    lane = lax.broadcasted_iota(jnp.int32, (ROWS, HD), 1)
    position = token - doc_starts(lens_ref, token)
    half = HD // 2
    angles = position.astype(jnp.float32) * inverse_frequency(
        jnp.where(lane < half, lane, lane - half)
    )
    cosine = jnp.cos(angles)
    sine = jnp.sin(angles)
    sine = jnp.where(lane < half, -sine, sine)
    copies[0].wait()
    copies[1].wait()
    gain = gain_ref[...]
    for h in range(KVH):
        values_f = key_ref[:, pl.ds(h * HD, HD)].astype(jnp.float32)
        inv_rms = lax.rsqrt(jnp.mean(values_f * values_f, axis=-1, keepdims=True) + NORM_EPS)
        normed = values_f * inv_rms * gain
        swapped = pltpu.roll(normed, half, 1)
        kv_ref[h, :, :HD] = (normed * cosine + swapped * sine).astype(jnp.bfloat16)
    copies[2].wait()
    for h in range(KVH):
        kv_ref[h, :, HD:] = value_ref[:, pl.ds(h * HD, HD)]


SMEM_SPEC = pl.BlockSpec(memory_space=pltpu.SMEM)
VMEM_SPEC = pl.BlockSpec(memory_space=pltpu.VMEM)
HBM_SPEC = pl.BlockSpec(memory_space=pltpu.HBM)
PARAMS = pltpu.CompilerParams(vmem_limit_bytes=VMEM_LIMIT)


def stay(array):
    return pltpu.with_memory_space_constraint(array, pltpu.HBM)


def prepare_keys(where, lens, key, value, gain):
    return pl.pallas_call(
        key_kernel,
        out_shape=jax.ShapeDtypeStruct((KVH, ROWS, 2 * HD), jnp.bfloat16),
        in_specs=[SMEM_SPEC, SMEM_SPEC, HBM_SPEC, HBM_SPEC, HBM_SPEC],
        out_specs=VMEM_SPEC,
        scratch_shapes=[
            pltpu.VMEM((ROWS, KVH * HD), jnp.bfloat16),
            pltpu.VMEM((ROWS, KVH * HD), jnp.bfloat16),
            pltpu.VMEM((1, HD), jnp.float32),
            pltpu.SemaphoreType.DMA((3,)),
        ],
        compiler_params=PARAMS,
        name="prepare_keys",
    )(where, stay(lens), stay(key), stay(value), stay(gain))


def query_kernel(where_ref, lens_ref, query_hbm, gain_ref, out_ref, query_ref, sems):
    def copy_of(h):
        piece = pl.ds(h * SHARE * HD, SHARE * HD)
        return pltpu.make_async_copy(
            query_hbm.at[0, :, piece], query_ref.at[:, piece], sems.at[h]
        )

    for h in range(KVH):
        copy_of(h).start()
    half = HD // 2
    lane = lax.broadcasted_iota(jnp.int32, (half, 2 * ROWS), 1)
    token = where_ref[0] * ROWS + jnp.where(lane < ROWS, lane, lane - ROWS)
    position = token - doc_starts(lens_ref, token)
    pair = lax.broadcasted_iota(jnp.int32, (half, 2 * ROWS), 0)
    angles = position.astype(jnp.float32) * inverse_frequency(pair)
    cosine = jnp.cos(angles)
    sine = jnp.sin(angles)
    gain = jnp.broadcast_to(gain_ref[...], (HD, HD)).T
    for h in range(KVH):
        copy_of(h).wait()
        for c in range(SHARE // 2):
            column = (h * SHARE + 2 * c) * HD
            both = jnp.concatenate(
                [query_ref[:, pl.ds(column, HD)], query_ref[:, pl.ds(column + HD, HD)]], axis=0
            )
            values_f = both.T.astype(jnp.float32)
            inv_rms = lax.rsqrt(jnp.mean(values_f * values_f, axis=0, keepdims=True) + NORM_EPS)
            normed = values_f * inv_rms * gain
            front, back = normed[:half], normed[half:]
            lanes = pl.ds(c * 2 * ROWS, 2 * ROWS)
            out_ref[h, :half, lanes] = (front * cosine - back * sine).astype(jnp.bfloat16)
            out_ref[h, half:, lanes] = (back * cosine + front * sine).astype(jnp.bfloat16)


def prepare_queries(where, lens, query, gain):
    return pl.pallas_call(
        query_kernel,
        out_shape=jax.ShapeDtypeStruct((KVH, HD, SHARE * ROWS), jnp.bfloat16),
        in_specs=[SMEM_SPEC, SMEM_SPEC, HBM_SPEC, VMEM_SPEC],
        out_specs=VMEM_SPEC,
        scratch_shapes=[
            pltpu.VMEM((ROWS, KVH * SHARE * HD), jnp.bfloat16),
            pltpu.SemaphoreType.DMA((KVH,)),
        ],
        compiler_params=PARAMS,
        cost_estimate=pl.CostEstimate(flops=10_000_000, bytes_accessed=4 << 20, transcendentals=0),
        name="prepare_queries",
    )(where, stay(lens), stay(query), stay(gain))


def visible_bias(where_ref, lens_ref, offsets):
    shape = (ROWS, 2 * ROWS)
    block = where_ref[0]
    lane = lax.broadcasted_iota(jnp.int32, shape, 1)
    token = block * ROWS + jnp.where(lane < ROWS, lane, lane - ROWS)
    start = doc_starts(lens_ref, token)
    row = lax.broadcasted_iota(jnp.int32, shape, 0)
    pieces = []
    for offset in offsets:
        source = (block - offset) * ROWS + row
        seen = (source >= start) & (source <= token)
        pieces.append(jnp.where(seen, 0.0, MASKED))
    return jnp.concatenate(pieces, axis=0)


def masked_scores(h, query_ref, parts, bias):
    keys = jnp.concatenate([p[:, :HD] for p in parts], axis=0)
    scores = jnp.dot(keys, query_ref[h], preferred_element_type=jnp.float32)
    return scores * (LOG2E / math.sqrt(HD)) + jnp.concatenate([bias] * (SHARE // 2), axis=1)


def mix_values(parts, weights):
    values = jnp.concatenate([p[:, HD:] for p in parts], axis=0)
    return lax.dot_general(
        values,
        weights.astype(jnp.bfloat16),
        (((0,), (0,)), ((), ())),
        preferred_element_type=jnp.float32,
    )


def early_kernel(offsets, where_ref, lens_ref, query_ref, *refs):
    blocks, (acc_ref, stat_ref) = refs[: len(offsets)], refs[len(offsets) :]
    bias = visible_bias(where_ref, lens_ref, offsets)
    for h in range(KVH):
        parts = [b[h] for b in blocks]
        scores = masked_scores(h, query_ref, parts, bias)
        top = jnp.max(scores, axis=0, keepdims=True)
        weights = jnp.exp2(scores - top)
        stat_ref[h, 0:1, :] = top
        stat_ref[h, 1:2, :] = jnp.sum(weights, axis=0, keepdims=True)
        acc_ref[h] = mix_values(parts, weights)


def late_kernel(offsets, where_ref, lens_ref, query_ref, acc_ref, stat_ref, cache_ref, *refs):
    count = len(offsets)
    blocks, other_ref = refs[:count], refs[count]
    out_hbm, cache_hbm, out_ref, sems, cache_sem = refs[count + 1 :]
    cache_copy = pltpu.make_async_copy(cache_ref, cache_hbm, cache_sem)
    cache_copy.start()
    bias = visible_bias(where_ref, lens_ref, offsets)
    own = where_ref[0]
    use_other = jnp.logical_and(own >= REACH, own < REACH + REACH // 2)
    copies = []
    for h in range(KVH):
        last = jnp.where(use_other, other_ref[h], blocks[-1][h])
        parts = [b[h] for b in blocks[:-1]] + [last]
        scores = masked_scores(h, query_ref, parts, bias)
        old_top = stat_ref[h, 0:1, :]
        top = jnp.maximum(old_top, jnp.max(scores, axis=0, keepdims=True))
        keep = jnp.exp2(old_top - top)
        weights = jnp.exp2(scores - top)
        denom = stat_ref[h, 1:2, :] * keep + jnp.sum(weights, axis=0, keepdims=True)
        mixed = acc_ref[h] * keep + mix_values(parts, weights)
        rounded = (mixed * (1.0 / denom)).astype(jnp.bfloat16)
        for c in range(SHARE // 2):
            both = rounded[:, c * 2 * ROWS : (c + 1) * 2 * ROWS].T
            column = (h * SHARE + 2 * c) * HD
            out_ref[:, pl.ds(column, HD)] = both[:ROWS]
            out_ref[:, pl.ds(column + HD, HD)] = both[ROWS:]
        piece = pl.ds(h * SHARE * HD, SHARE * HD)
        copies.append(
            pltpu.make_async_copy(out_ref.at[:, piece], out_hbm.at[0, :, piece], sems.at[h])
        )
        copies[-1].start()
    for copy in copies:
        copy.wait()
    cache_copy.wait()


def attention_cost(count):
    return pl.CostEstimate(
        flops=4 * KVH * SHARE * ROWS * ROWS * HD * count,
        bytes_accessed=4 << 20,
        transcendentals=KVH * SHARE * ROWS * ROWS * count,
    )


def attend_early(offsets, where, lens, query, blocks):
    count = len(offsets)
    return pl.pallas_call(
        lambda *refs: early_kernel(offsets, *refs),
        out_shape=(
            jax.ShapeDtypeStruct((KVH, HD, SHARE * ROWS), jnp.float32),
            jax.ShapeDtypeStruct((KVH, 8, SHARE * ROWS), jnp.float32),
        ),
        in_specs=[SMEM_SPEC, SMEM_SPEC] + [VMEM_SPEC] * (1 + count),
        out_specs=(VMEM_SPEC, VMEM_SPEC),
        compiler_params=PARAMS,
        cost_estimate=attention_cost(count),
        name="attend_early",
    )(where, stay(lens), query, *blocks)


def attend_late(offsets, where, lens, query, acc, stat, cache, blocks):
    count = len(offsets)
    return pl.pallas_call(
        lambda *refs: late_kernel(offsets, *refs),
        out_shape=(
            jax.ShapeDtypeStruct((1, ROWS, KVH * SHARE * HD), jnp.bfloat16),
            jax.ShapeDtypeStruct(cache.shape, cache.dtype),
        ),
        in_specs=[SMEM_SPEC, SMEM_SPEC] + [VMEM_SPEC] * (4 + count + 1),
        out_specs=(HBM_SPEC, HBM_SPEC),
        scratch_shapes=[
            pltpu.VMEM((ROWS, KVH * SHARE * HD), jnp.bfloat16),
            pltpu.SemaphoreType.DMA((KVH,)),
            pltpu.SemaphoreType.DMA(()),
        ],
        compiler_params=PARAMS,
        cost_estimate=attention_cost(count),
        name="attend_late",
    )(where, stay(lens), query, acc, stat, cache, *blocks)


def pages_kernel(where_ref, kv_ref, out_ref):
    place = jnp.bitwise_and(where_ref[0], KVH - 1)
    for h in range(KVH):
        out_ref[h] = kv_ref[jnp.bitwise_xor(place, h)]


def order_pages(where, kv):
    return pl.pallas_call(
        pages_kernel,
        out_shape=jax.ShapeDtypeStruct((KVH, ROWS, 2 * HD), jnp.bfloat16),
        in_specs=[SMEM_SPEC, VMEM_SPEC],
        out_specs=VMEM_SPEC,
        compiler_params=PARAMS,
        name="order_pages",
    )(where, kv)


def plus_pairs(count, step):
    receivers = range(step, count)
    if step == REACH // 2:
        receivers = [r for r in receivers if r % REACH >= step]
    return [(r - 1, r) for r in receivers]


def diagonal_pairs(count):
    return [(i, i + REACH - 1) for i in range(count - REACH + 1)] + [
        (REACH + 1 + i, i) for i in range(2)
    ]


def partner_pairs(count):
    return [(i, i + REACH) for i in range(count - REACH)]


def minus_pairs(count, step):
    if step == REACH // 2:
        return [(r + 1, r) for r in range(REACH, REACH + step)]
    receivers = list(range(REACH - step, count)) + list(range(0, 3 - step))
    return [((r + 1) % count, r) for r in receivers]


def slot_pairs(seqs, groups):
    pairs = []
    spread = groups // KVH
    for s in range(seqs):
        repeat, place = divmod(s, KVH)
        for g in range(groups):
            slot, page = divmod(g, spread)
            entry = (slot ^ place) * 2 + repeat
            pairs.append((s * groups + g, entry * groups + place * spread + page))
    return pairs


def body(query_proj, key_proj, value_proj, query_gain, key_gain, doc_lengths):
    seqs = lax.axis_size("seq")
    groups = lax.axis_size("group")
    where = lax.axis_index("seq").astype(jnp.int32).reshape(1)
    kv = prepare_keys(where, doc_lengths, key_proj, value_proj, key_gain.reshape(1, HD))
    minus1 = lax.ppermute(kv, "seq", plus_pairs(seqs, 1))
    minus7 = lax.ppermute(kv, "seq", diagonal_pairs(seqs))
    minus8 = lax.ppermute(kv, "seq", partner_pairs(seqs))
    pages = order_pages(where, kv).reshape(groups, PAGE, 2 * HD)
    mine = lax.all_to_all(pages, "group", split_axis=0, concat_axis=0, tiled=True)
    minus2 = lax.ppermute(minus1, "seq", plus_pairs(seqs, 2))
    minus6 = lax.ppermute(minus7, "seq", minus_pairs(seqs, 2))
    minus1, later = lax.optimization_barrier((minus1, where))
    query = prepare_queries(later, doc_lengths, query_proj, query_gain.reshape(1, HD))
    minus2, query, mine = lax.optimization_barrier((minus2, query, mine))
    minus3 = lax.ppermute(minus2, "seq", plus_pairs(seqs, 3))
    minus5 = lax.ppermute(minus6, "seq", minus_pairs(seqs, 3))
    cache = lax.ppermute(mine, ("seq", "group"), slot_pairs(seqs, groups))
    plus4 = lax.ppermute(minus3, "seq", plus_pairs(seqs, 4))
    minus4 = lax.ppermute(minus5, "seq", minus_pairs(seqs, 4))
    acc, stat = attend_early(
        (0, 1, 7, 8, 2, 6, 3, 5),
        where,
        doc_lengths,
        query,
        [kv, minus1, minus7, minus8, minus2, minus6, minus3, minus5],
    )
    attended, cache = attend_late(
        (4,), where, doc_lengths, query, acc, stat, cache, [plus4, minus4]
    )
    return attended, cache.reshape(1, 1, groups, 1, PAGE, 2 * HD)


def solution(mesh):
    rows = P("group", "seq", None)
    in_specs = (rows, rows, rows, P(), P(), P("group", None))
    out_specs = (rows, P("seq", "group", None, None, None, None))
    return jax.shard_map(body, mesh=mesh, in_specs=in_specs, out_specs=out_specs, check_vma=False)
```

```python
import math

import jax
import jax.numpy as jnp
from jax import lax
from jax.experimental import pallas as pl
from jax.experimental.pallas import tpu as pltpu
from jax.sharding import PartitionSpec as P

PAGE = 16
NORM_EPS = 1e-06
ROPE_BASE = 1000000.0
MASKED = -1e30
HD = 128
KVH = 8
SHARE = 8
ROWS = 64
REACH = 8
LOG2E = 1.4426950408889634
VMEM_LIMIT = 20 * 1024 * 1024


def doc_starts(lens_ref, token):
    start = jnp.zeros(token.shape, jnp.int32)
    end = jnp.int32(0)
    for d in range(lens_ref.shape[1]):
        length = lens_ref[0, d]
        end = end + length
        start = start + jnp.where(end <= token, length, 0)
    return start


def inverse_frequency(pair):
    return jnp.exp(pair.astype(jnp.float32) * (-2.0 * math.log(ROPE_BASE) / HD))


def key_kernel(
    where_ref, lens_ref, key_hbm, value_hbm, gain_hbm, kv_ref, key_ref, value_ref, gain_ref, sems
):
    copies = [
        pltpu.make_async_copy(key_hbm.at[0], key_ref, sems.at[0]),
        pltpu.make_async_copy(gain_hbm, gain_ref, sems.at[1]),
        pltpu.make_async_copy(value_hbm.at[0], value_ref, sems.at[2]),
    ]
    for copy in copies:
        copy.start()
    token = where_ref[0] * ROWS + lax.broadcasted_iota(jnp.int32, (ROWS, HD), 0)
    lane = lax.broadcasted_iota(jnp.int32, (ROWS, HD), 1)
    position = token - doc_starts(lens_ref, token)
    half = HD // 2
    angles = position.astype(jnp.float32) * inverse_frequency(
        jnp.where(lane < half, lane, lane - half)
    )
    cosine = jnp.cos(angles)
    sine = jnp.sin(angles)
    sine = jnp.where(lane < half, -sine, sine)
    copies[0].wait()
    copies[1].wait()
    gain = gain_ref[...]
    for h in range(KVH):
        values_f = key_ref[:, pl.ds(h * HD, HD)].astype(jnp.float32)
        inv_rms = lax.rsqrt(jnp.mean(values_f * values_f, axis=-1, keepdims=True) + NORM_EPS)
        normed = values_f * inv_rms * gain
        swapped = pltpu.roll(normed, half, 1)
        kv_ref[h, :, :HD] = (normed * cosine + swapped * sine).astype(jnp.bfloat16)
    copies[2].wait()
    for h in range(KVH):
        kv_ref[h, :, HD:] = value_ref[:, pl.ds(h * HD, HD)]


SMEM_SPEC = pl.BlockSpec(memory_space=pltpu.SMEM)
VMEM_SPEC = pl.BlockSpec(memory_space=pltpu.VMEM)
HBM_SPEC = pl.BlockSpec(memory_space=pltpu.HBM)
PARAMS = pltpu.CompilerParams(vmem_limit_bytes=VMEM_LIMIT)


def stay(array):
    return pltpu.with_memory_space_constraint(array, pltpu.HBM)


def prepare_keys(where, lens, key, value, gain):
    return pl.pallas_call(
        key_kernel,
        out_shape=jax.ShapeDtypeStruct((KVH, ROWS, 2 * HD), jnp.bfloat16),
        in_specs=[SMEM_SPEC, SMEM_SPEC, HBM_SPEC, HBM_SPEC, HBM_SPEC],
        out_specs=VMEM_SPEC,
        scratch_shapes=[
            pltpu.VMEM((ROWS, KVH * HD), jnp.bfloat16),
            pltpu.VMEM((ROWS, KVH * HD), jnp.bfloat16),
            pltpu.VMEM((1, HD), jnp.float32),
            pltpu.SemaphoreType.DMA((3,)),
        ],
        compiler_params=PARAMS,
        name="prepare_keys",
    )(where, stay(lens), stay(key), stay(value), stay(gain))


def query_kernel(where_ref, lens_ref, query_hbm, gain_ref, out_ref, query_ref, sems):
    def copy_of(h):
        piece = pl.ds(h * SHARE * HD, SHARE * HD)
        return pltpu.make_async_copy(
            query_hbm.at[0, :, piece], query_ref.at[:, piece], sems.at[h]
        )

    for h in range(KVH):
        copy_of(h).start()
    half = HD // 2
    lane = lax.broadcasted_iota(jnp.int32, (half, 2 * ROWS), 1)
    token = where_ref[0] * ROWS + jnp.where(lane < ROWS, lane, lane - ROWS)
    position = token - doc_starts(lens_ref, token)
    pair = lax.broadcasted_iota(jnp.int32, (half, 2 * ROWS), 0)
    angles = position.astype(jnp.float32) * inverse_frequency(pair)
    cosine = jnp.cos(angles)
    sine = jnp.sin(angles)
    gain = jnp.broadcast_to(gain_ref[...], (HD, HD)).T
    for h in range(KVH):
        copy_of(h).wait()
        for c in range(SHARE // 2):
            column = (h * SHARE + 2 * c) * HD
            both = jnp.concatenate(
                [query_ref[:, pl.ds(column, HD)], query_ref[:, pl.ds(column + HD, HD)]], axis=0
            )
            values_f = both.T.astype(jnp.float32)
            inv_rms = lax.rsqrt(jnp.mean(values_f * values_f, axis=0, keepdims=True) + NORM_EPS)
            normed = values_f * inv_rms * gain
            front, back = normed[:half], normed[half:]
            lanes = pl.ds(c * 2 * ROWS, 2 * ROWS)
            out_ref[h, :half, lanes] = (front * cosine - back * sine).astype(jnp.bfloat16)
            out_ref[h, half:, lanes] = (back * cosine + front * sine).astype(jnp.bfloat16)


def prepare_queries(where, lens, query, gain):
    return pl.pallas_call(
        query_kernel,
        out_shape=jax.ShapeDtypeStruct((KVH, HD, SHARE * ROWS), jnp.bfloat16),
        in_specs=[SMEM_SPEC, SMEM_SPEC, HBM_SPEC, VMEM_SPEC],
        out_specs=VMEM_SPEC,
        scratch_shapes=[
            pltpu.VMEM((ROWS, KVH * SHARE * HD), jnp.bfloat16),
            pltpu.SemaphoreType.DMA((KVH,)),
        ],
        compiler_params=PARAMS,
        cost_estimate=pl.CostEstimate(flops=10_000_000, bytes_accessed=4 << 20, transcendentals=0),
        name="prepare_queries",
    )(where, stay(lens), stay(query), stay(gain))


def visible_bias(where_ref, lens_ref, offsets):
    shape = (ROWS, 2 * ROWS)
    block = where_ref[0]
    lane = lax.broadcasted_iota(jnp.int32, shape, 1)
    token = block * ROWS + jnp.where(lane < ROWS, lane, lane - ROWS)
    start = doc_starts(lens_ref, token)
    row = lax.broadcasted_iota(jnp.int32, shape, 0)
    pieces = []
    for offset in offsets:
        source = (block - offset) * ROWS + row
        seen = (source >= start) & (source <= token)
        pieces.append(jnp.where(seen, 0.0, MASKED))
    return jnp.concatenate(pieces, axis=0)


def masked_scores(h, query_ref, parts, bias):
    keys = jnp.concatenate([p[:, :HD] for p in parts], axis=0)
    scores = jnp.dot(keys, query_ref[h], preferred_element_type=jnp.float32)
    return scores * (LOG2E / math.sqrt(HD)) + jnp.concatenate([bias] * (SHARE // 2), axis=1)


def mix_values(parts, weights):
    values = jnp.concatenate([p[:, HD:] for p in parts], axis=0)
    return lax.dot_general(
        values,
        weights.astype(jnp.bfloat16),
        (((0,), (0,)), ((), ())),
        preferred_element_type=jnp.float32,
    )


def early_kernel(offsets, where_ref, lens_ref, query_ref, *refs):
    blocks, (acc_ref, stat_ref) = refs[: len(offsets)], refs[len(offsets) :]
    bias = visible_bias(where_ref, lens_ref, offsets)
    for h in range(KVH):
        parts = [b[h] for b in blocks]
        scores = masked_scores(h, query_ref, parts, bias)
        top = jnp.max(scores, axis=0, keepdims=True)
        weights = jnp.exp2(scores - top)
        stat_ref[h, 0:1, :] = top
        stat_ref[h, 1:2, :] = jnp.sum(weights, axis=0, keepdims=True)
        acc_ref[h] = mix_values(parts, weights)


def late_kernel(offsets, where_ref, lens_ref, query_ref, acc_ref, stat_ref, cache_ref, *refs):
    count = len(offsets)
    blocks, other_ref = refs[:count], refs[count]
    out_hbm, cache_hbm, out_ref, sems, cache_sem = refs[count + 1 :]
    cache_copy = pltpu.make_async_copy(cache_ref, cache_hbm, cache_sem)
    cache_copy.start()
    bias = visible_bias(where_ref, lens_ref, offsets)
    own = where_ref[0]
    use_other = jnp.logical_and(own >= REACH, own < REACH + REACH // 2)
    copies = []
    for h in range(KVH):
        last = jnp.where(use_other, other_ref[h], blocks[-1][h])
        parts = [b[h] for b in blocks[:-1]] + [last]
        scores = masked_scores(h, query_ref, parts, bias)
        old_top = stat_ref[h, 0:1, :]
        top = jnp.maximum(old_top, jnp.max(scores, axis=0, keepdims=True))
        keep = jnp.exp2(old_top - top)
        weights = jnp.exp2(scores - top)
        denom = stat_ref[h, 1:2, :] * keep + jnp.sum(weights, axis=0, keepdims=True)
        mixed = acc_ref[h] * keep + mix_values(parts, weights)
        rounded = (mixed * (1.0 / denom)).astype(jnp.bfloat16)
        for c in range(SHARE // 2):
            both = rounded[:, c * 2 * ROWS : (c + 1) * 2 * ROWS].T
            column = (h * SHARE + 2 * c) * HD
            out_ref[:, pl.ds(column, HD)] = both[:ROWS]
            out_ref[:, pl.ds(column + HD, HD)] = both[ROWS:]
        piece = pl.ds(h * SHARE * HD, SHARE * HD)
        copies.append(
            pltpu.make_async_copy(out_ref.at[:, piece], out_hbm.at[0, :, piece], sems.at[h])
        )
        copies[-1].start()
    for copy in copies:
        copy.wait()
    cache_copy.wait()


def attention_cost(count):
    return pl.CostEstimate(
        flops=4 * KVH * SHARE * ROWS * ROWS * HD * count,
        bytes_accessed=4 << 20,
        transcendentals=KVH * SHARE * ROWS * ROWS * count,
    )


def attend_early(offsets, where, lens, query, blocks):
    count = len(offsets)
    return pl.pallas_call(
        lambda *refs: early_kernel(offsets, *refs),
        out_shape=(
            jax.ShapeDtypeStruct((KVH, HD, SHARE * ROWS), jnp.float32),
            jax.ShapeDtypeStruct((KVH, 8, SHARE * ROWS), jnp.float32),
        ),
        in_specs=[SMEM_SPEC, SMEM_SPEC] + [VMEM_SPEC] * (1 + count),
        out_specs=(VMEM_SPEC, VMEM_SPEC),
        compiler_params=PARAMS,
        cost_estimate=attention_cost(count),
        name="attend_early",
    )(where, stay(lens), query, *blocks)


def attend_late(offsets, where, lens, query, acc, stat, cache, blocks):
    count = len(offsets)
    return pl.pallas_call(
        lambda *refs: late_kernel(offsets, *refs),
        out_shape=(
            jax.ShapeDtypeStruct((1, ROWS, KVH * SHARE * HD), jnp.bfloat16),
            jax.ShapeDtypeStruct(cache.shape, cache.dtype),
        ),
        in_specs=[SMEM_SPEC, SMEM_SPEC] + [VMEM_SPEC] * (4 + count + 1),
        out_specs=(HBM_SPEC, HBM_SPEC),
        scratch_shapes=[
            pltpu.VMEM((ROWS, KVH * SHARE * HD), jnp.bfloat16),
            pltpu.SemaphoreType.DMA((KVH,)),
            pltpu.SemaphoreType.DMA(()),
        ],
        compiler_params=PARAMS,
        cost_estimate=attention_cost(count),
        name="attend_late",
    )(where, stay(lens), query, acc, stat, cache, *blocks)


def pages_kernel(where_ref, kv_ref, out_ref):
    place = jnp.bitwise_and(where_ref[0], KVH - 1)
    for h in range(KVH):
        out_ref[h] = kv_ref[jnp.bitwise_xor(place, h)]


def order_pages(where, kv):
    return pl.pallas_call(
        pages_kernel,
        out_shape=jax.ShapeDtypeStruct((KVH, ROWS, 2 * HD), jnp.bfloat16),
        in_specs=[SMEM_SPEC, VMEM_SPEC],
        out_specs=VMEM_SPEC,
        compiler_params=PARAMS,
        name="order_pages",
    )(where, kv)


def plus_pairs(count, step):
    receivers = range(step, count)
    if step == REACH // 2:
        receivers = [r for r in receivers if r % REACH >= step]
    return [(r - 1, r) for r in receivers]


def diagonal_pairs(count):
    return [(i, i + REACH - 1) for i in range(count - REACH + 1)] + [
        (REACH + 1 + i, i) for i in range(2)
    ]


def partner_pairs(count):
    return [(i, i + REACH) for i in range(count - REACH)]


def minus_pairs(count, step):
    if step == REACH // 2:
        return [(r + 1, r) for r in range(REACH, REACH + step)]
    receivers = list(range(REACH - step, count)) + list(range(0, 3 - step))
    return [((r + 1) % count, r) for r in receivers]


def slot_pairs(seqs, groups):
    pairs = []
    spread = groups // KVH
    for s in range(seqs):
        repeat, place = divmod(s, KVH)
        for g in range(groups):
            slot, page = divmod(g, spread)
            entry = (slot ^ place) * 2 + repeat
            pairs.append((s * groups + g, entry * groups + place * spread + page))
    return pairs


def body(query_proj, key_proj, value_proj, query_gain, key_gain, doc_lengths):
    seqs = lax.axis_size("seq")
    groups = lax.axis_size("group")
    where = lax.axis_index("seq").astype(jnp.int32).reshape(1)
    kv = prepare_keys(where, doc_lengths, key_proj, value_proj, key_gain.reshape(1, HD))
    minus1 = lax.ppermute(kv, "seq", plus_pairs(seqs, 1))
    minus7 = lax.ppermute(kv, "seq", diagonal_pairs(seqs))
    pages = order_pages(where, kv).reshape(groups, PAGE, 2 * HD)
    mine = lax.all_to_all(pages, "group", split_axis=0, concat_axis=0, tiled=True)
    minus2 = lax.ppermute(minus1, "seq", plus_pairs(seqs, 2))
    minus6 = lax.ppermute(minus7, "seq", minus_pairs(seqs, 2))
    minus1, later = lax.optimization_barrier((minus1, where))
    query = prepare_queries(later, doc_lengths, query_proj, query_gain.reshape(1, HD))
    minus2, query, mine = lax.optimization_barrier((minus2, query, mine))
    minus3 = lax.ppermute(minus2, "seq", plus_pairs(seqs, 3))
    minus5 = lax.ppermute(minus6, "seq", minus_pairs(seqs, 3))
    cache = lax.ppermute(mine, ("seq", "group"), slot_pairs(seqs, groups))
    minus3, kv_again = lax.optimization_barrier((minus3, kv))
    plus4 = lax.ppermute(minus3, "seq", plus_pairs(seqs, 4))
    minus4 = lax.ppermute(minus5, "seq", minus_pairs(seqs, 4))
    acc, stat = attend_early(
        (0, 1, 7, 2, 6, 3, 5),
        where,
        doc_lengths,
        query,
        [kv, minus1, minus7, minus2, minus6, minus3, minus5],
    )
    minus8 = lax.ppermute(kv_again, "seq", partner_pairs(seqs))
    attended, cache = attend_late(
        (8, 4), where, doc_lengths, query, acc, stat, cache, [minus8, plus4, minus4]
    )
    return attended, cache.reshape(1, 1, groups, 1, PAGE, 2 * HD)


def solution(mesh):
    rows = P("group", "seq", None)
    in_specs = (rows, rows, rows, P(), P(), P("group", None))
    out_specs = (rows, P("seq", "group", None, None, None, None))
    return jax.shard_map(body, mesh=mesh, in_specs=in_specs, out_specs=out_specs, check_vma=False)
```

```python
import math

import jax
import jax.numpy as jnp
from jax import lax
from jax.experimental import pallas as pl
from jax.experimental.pallas import tpu as pltpu
from jax.sharding import PartitionSpec as P

PAGE = 16
NORM_EPS = 1e-06
ROPE_BASE = 1000000.0
MASKED = -1e30
HD = 128
KVH = 8
SHARE = 8
ROWS = 64
REACH = 8
LOG2E = 1.4426950408889634
VMEM_LIMIT = 20 * 1024 * 1024


def doc_starts(lens_ref, token):
    start = jnp.zeros(token.shape, jnp.int32)
    end = jnp.int32(0)
    for d in range(lens_ref.shape[1]):
        length = lens_ref[0, d]
        end = end + length
        start = start + jnp.where(end <= token, length, 0)
    return start


def inverse_frequency(pair):
    return jnp.exp(pair.astype(jnp.float32) * (-2.0 * math.log(ROPE_BASE) / HD))


def key_kernel(
    where_ref, lens_ref, key_hbm, value_hbm, gain_hbm, kv_ref, key_ref, gain_ref, sems
):
    copies = [
        pltpu.make_async_copy(key_hbm.at[0], key_ref, sems.at[0]),
        pltpu.make_async_copy(gain_hbm, gain_ref, sems.at[1]),
    ] + [
        pltpu.make_async_copy(
            value_hbm.at[0, :, pl.ds(h * HD, HD)], kv_ref.at[h, :, pl.ds(HD, HD)], sems.at[2 + h]
        )
        for h in range(KVH)
    ]
    for copy in copies:
        copy.start()
    token = where_ref[0] * ROWS + lax.broadcasted_iota(jnp.int32, (ROWS, HD), 0)
    lane = lax.broadcasted_iota(jnp.int32, (ROWS, HD), 1)
    position = token - doc_starts(lens_ref, token)
    half = HD // 2
    angles = position.astype(jnp.float32) * inverse_frequency(
        jnp.where(lane < half, lane, lane - half)
    )
    cosine = jnp.cos(angles)
    sine = jnp.sin(angles)
    sine = jnp.where(lane < half, -sine, sine)
    copies[0].wait()
    copies[1].wait()
    gain = gain_ref[...]
    for h in range(KVH):
        values_f = key_ref[:, pl.ds(h * HD, HD)].astype(jnp.float32)
        inv_rms = lax.rsqrt(jnp.mean(values_f * values_f, axis=-1, keepdims=True) + NORM_EPS)
        normed = values_f * inv_rms * gain
        swapped = pltpu.roll(normed, half, 1)
        kv_ref[h, :, :HD] = (normed * cosine + swapped * sine).astype(jnp.bfloat16)
    for copy in copies[2:]:
        copy.wait()


SMEM_SPEC = pl.BlockSpec(memory_space=pltpu.SMEM)
VMEM_SPEC = pl.BlockSpec(memory_space=pltpu.VMEM)
HBM_SPEC = pl.BlockSpec(memory_space=pltpu.HBM)
PARAMS = pltpu.CompilerParams(vmem_limit_bytes=VMEM_LIMIT)


def stay(array):
    return pltpu.with_memory_space_constraint(array, pltpu.HBM)


def prepare_keys(where, lens, key, value, gain):
    return pl.pallas_call(
        key_kernel,
        out_shape=jax.ShapeDtypeStruct((KVH, ROWS, 2 * HD), jnp.bfloat16),
        in_specs=[SMEM_SPEC, SMEM_SPEC, HBM_SPEC, HBM_SPEC, HBM_SPEC],
        out_specs=VMEM_SPEC,
        scratch_shapes=[
            pltpu.VMEM((ROWS, KVH * HD), jnp.bfloat16),
            pltpu.VMEM((1, HD), jnp.float32),
            pltpu.SemaphoreType.DMA((2 + KVH,)),
        ],
        compiler_params=PARAMS,
        name="prepare_keys",
    )(where, stay(lens), stay(key), stay(value), stay(gain))


def query_kernel(where_ref, lens_ref, query_hbm, gain_ref, out_ref, query_ref, sems):
    def copy_of(h):
        piece = pl.ds(h * SHARE * HD, SHARE * HD)
        return pltpu.make_async_copy(
            query_hbm.at[0, :, piece], query_ref.at[:, piece], sems.at[h]
        )

    for h in range(KVH):
        copy_of(h).start()
    half = HD // 2
    lane = lax.broadcasted_iota(jnp.int32, (half, 2 * ROWS), 1)
    token = where_ref[0] * ROWS + jnp.where(lane < ROWS, lane, lane - ROWS)
    position = token - doc_starts(lens_ref, token)
    pair = lax.broadcasted_iota(jnp.int32, (half, 2 * ROWS), 0)
    angles = position.astype(jnp.float32) * inverse_frequency(pair)
    cosine = jnp.cos(angles)
    sine = jnp.sin(angles)
    gain = jnp.broadcast_to(gain_ref[...], (HD, HD)).T
    for h in range(KVH):
        copy_of(h).wait()
        for c in range(SHARE // 2):
            column = (h * SHARE + 2 * c) * HD
            both = jnp.concatenate(
                [query_ref[:, pl.ds(column, HD)], query_ref[:, pl.ds(column + HD, HD)]], axis=0
            )
            values_f = both.T.astype(jnp.float32)
            inv_rms = lax.rsqrt(jnp.mean(values_f * values_f, axis=0, keepdims=True) + NORM_EPS)
            normed = values_f * inv_rms * gain
            front, back = normed[:half], normed[half:]
            lanes = pl.ds(c * 2 * ROWS, 2 * ROWS)
            out_ref[h, :half, lanes] = (front * cosine - back * sine).astype(jnp.bfloat16)
            out_ref[h, half:, lanes] = (back * cosine + front * sine).astype(jnp.bfloat16)


def prepare_queries(where, lens, query, gain):
    return pl.pallas_call(
        query_kernel,
        out_shape=jax.ShapeDtypeStruct((KVH, HD, SHARE * ROWS), jnp.bfloat16),
        in_specs=[SMEM_SPEC, SMEM_SPEC, HBM_SPEC, VMEM_SPEC],
        out_specs=VMEM_SPEC,
        scratch_shapes=[
            pltpu.VMEM((ROWS, KVH * SHARE * HD), jnp.bfloat16),
            pltpu.SemaphoreType.DMA((KVH,)),
        ],
        compiler_params=PARAMS,
        cost_estimate=pl.CostEstimate(flops=10_000_000, bytes_accessed=4 << 20, transcendentals=0),
        name="prepare_queries",
    )(where, stay(lens), stay(query), stay(gain))


def visible_bias(where_ref, lens_ref, offsets):
    shape = (ROWS, 2 * ROWS)
    block = where_ref[0]
    lane = lax.broadcasted_iota(jnp.int32, shape, 1)
    token = block * ROWS + jnp.where(lane < ROWS, lane, lane - ROWS)
    start = doc_starts(lens_ref, token)
    row = lax.broadcasted_iota(jnp.int32, shape, 0)
    pieces = []
    for offset in offsets:
        source = (block - offset) * ROWS + row
        seen = (source >= start) & (source <= token)
        pieces.append(jnp.where(seen, 0.0, MASKED))
    return jnp.concatenate(pieces, axis=0)


def masked_scores(h, query_ref, parts, bias):
    keys = jnp.concatenate([p[:, :HD] for p in parts], axis=0)
    scores = jnp.dot(keys, query_ref[h], preferred_element_type=jnp.float32)
    return scores * (LOG2E / math.sqrt(HD)) + jnp.concatenate([bias] * (SHARE // 2), axis=1)


def mix_values(parts, weights):
    values = jnp.concatenate([p[:, HD:] for p in parts], axis=0)
    return lax.dot_general(
        values,
        weights.astype(jnp.bfloat16),
        (((0,), (0,)), ((), ())),
        preferred_element_type=jnp.float32,
    )


def early_kernel(offsets, where_ref, lens_ref, query_ref, *refs):
    blocks, (acc_ref, stat_ref) = refs[: len(offsets)], refs[len(offsets) :]
    bias = visible_bias(where_ref, lens_ref, offsets)
    for h in range(KVH):
        parts = [b[h] for b in blocks]
        scores = masked_scores(h, query_ref, parts, bias)
        top = jnp.max(scores, axis=0, keepdims=True)
        weights = jnp.exp2(scores - top)
        stat_ref[h, 0:1, :] = top
        stat_ref[h, 1:2, :] = jnp.sum(weights, axis=0, keepdims=True)
        acc_ref[h] = mix_values(parts, weights)


def late_kernel(offsets, where_ref, lens_ref, query_ref, acc_ref, stat_ref, cache_ref, *refs):
    count = len(offsets)
    blocks, other_ref = refs[:count], refs[count]
    out_hbm, cache_hbm, out_ref, sems, cache_sem = refs[count + 1 :]
    cache_copy = pltpu.make_async_copy(cache_ref, cache_hbm, cache_sem)
    cache_copy.start()
    bias = visible_bias(where_ref, lens_ref, offsets)
    own = where_ref[0]
    use_other = jnp.logical_and(own >= REACH, own < REACH + REACH // 2)
    copies = []
    for h in range(KVH):
        last = jnp.where(use_other, other_ref[h], blocks[-1][h])
        parts = [b[h] for b in blocks[:-1]] + [last]
        scores = masked_scores(h, query_ref, parts, bias)
        old_top = stat_ref[h, 0:1, :]
        top = jnp.maximum(old_top, jnp.max(scores, axis=0, keepdims=True))
        keep = jnp.exp2(old_top - top)
        weights = jnp.exp2(scores - top)
        denom = stat_ref[h, 1:2, :] * keep + jnp.sum(weights, axis=0, keepdims=True)
        mixed = acc_ref[h] * keep + mix_values(parts, weights)
        rounded = (mixed * (1.0 / denom)).astype(jnp.bfloat16)
        for c in range(SHARE // 2):
            both = rounded[:, c * 2 * ROWS : (c + 1) * 2 * ROWS].T
            column = (h * SHARE + 2 * c) * HD
            out_ref[:, pl.ds(column, HD)] = both[:ROWS]
            out_ref[:, pl.ds(column + HD, HD)] = both[ROWS:]
        piece = pl.ds(h * SHARE * HD, SHARE * HD)
        copies.append(
            pltpu.make_async_copy(out_ref.at[:, piece], out_hbm.at[0, :, piece], sems.at[h])
        )
        copies[-1].start()
    for copy in copies:
        copy.wait()
    cache_copy.wait()


def attention_cost(count):
    return pl.CostEstimate(
        flops=4 * KVH * SHARE * ROWS * ROWS * HD * count,
        bytes_accessed=4 << 20,
        transcendentals=KVH * SHARE * ROWS * ROWS * count,
    )


def attend_early(offsets, where, lens, query, blocks):
    count = len(offsets)
    return pl.pallas_call(
        lambda *refs: early_kernel(offsets, *refs),
        out_shape=(
            jax.ShapeDtypeStruct((KVH, HD, SHARE * ROWS), jnp.float32),
            jax.ShapeDtypeStruct((KVH, 8, SHARE * ROWS), jnp.float32),
        ),
        in_specs=[SMEM_SPEC, SMEM_SPEC] + [VMEM_SPEC] * (1 + count),
        out_specs=(VMEM_SPEC, VMEM_SPEC),
        compiler_params=PARAMS,
        cost_estimate=attention_cost(count),
        name="attend_early",
    )(where, stay(lens), query, *blocks)


def attend_late(offsets, where, lens, query, acc, stat, cache, blocks):
    count = len(offsets)
    return pl.pallas_call(
        lambda *refs: late_kernel(offsets, *refs),
        out_shape=(
            jax.ShapeDtypeStruct((1, ROWS, KVH * SHARE * HD), jnp.bfloat16),
            jax.ShapeDtypeStruct(cache.shape, cache.dtype),
        ),
        in_specs=[SMEM_SPEC, SMEM_SPEC] + [VMEM_SPEC] * (4 + count + 1),
        out_specs=(HBM_SPEC, HBM_SPEC),
        scratch_shapes=[
            pltpu.VMEM((ROWS, KVH * SHARE * HD), jnp.bfloat16),
            pltpu.SemaphoreType.DMA((KVH,)),
            pltpu.SemaphoreType.DMA(()),
        ],
        compiler_params=PARAMS,
        cost_estimate=attention_cost(count),
        name="attend_late",
    )(where, stay(lens), query, acc, stat, cache, *blocks)


def pages_kernel(where_ref, kv_ref, out_ref):
    place = jnp.bitwise_and(where_ref[0], KVH - 1)
    for h in range(KVH):
        out_ref[h] = kv_ref[jnp.bitwise_xor(place, h)]


def order_pages(where, kv):
    return pl.pallas_call(
        pages_kernel,
        out_shape=jax.ShapeDtypeStruct((KVH, ROWS, 2 * HD), jnp.bfloat16),
        in_specs=[SMEM_SPEC, VMEM_SPEC],
        out_specs=VMEM_SPEC,
        compiler_params=PARAMS,
        name="order_pages",
    )(where, kv)


def plus_pairs(count, step):
    receivers = range(step, count)
    if step == REACH // 2:
        receivers = [r for r in receivers if r % REACH >= step]
    return [(r - 1, r) for r in receivers]


def diagonal_pairs(count):
    return [(i, i + REACH - 1) for i in range(count - REACH + 1)] + [
        (REACH + 1 + i, i) for i in range(2)
    ]


def partner_pairs(count):
    return [(i, i + REACH) for i in range(count - REACH)]


def minus_pairs(count, step):
    if step == REACH // 2:
        return [(r + 1, r) for r in range(REACH, REACH + step)]
    receivers = list(range(REACH - step, count)) + list(range(0, 3 - step))
    return [((r + 1) % count, r) for r in receivers]


def slot_pairs(seqs, groups):
    pairs = []
    spread = groups // KVH
    for s in range(seqs):
        repeat, place = divmod(s, KVH)
        for g in range(groups):
            slot, page = divmod(g, spread)
            entry = (slot ^ place) * 2 + repeat
            pairs.append((s * groups + g, entry * groups + place * spread + page))
    return pairs


def body(query_proj, key_proj, value_proj, query_gain, key_gain, doc_lengths):
    seqs = lax.axis_size("seq")
    groups = lax.axis_size("group")
    where = lax.axis_index("seq").astype(jnp.int32).reshape(1)
    kv = prepare_keys(where, doc_lengths, key_proj, value_proj, key_gain.reshape(1, HD))
    minus1 = lax.ppermute(kv, "seq", plus_pairs(seqs, 1))
    minus7 = lax.ppermute(kv, "seq", diagonal_pairs(seqs))
    pages = order_pages(where, kv).reshape(groups, PAGE, 2 * HD)
    mine = lax.all_to_all(pages, "group", split_axis=0, concat_axis=0, tiled=True)
    minus2 = lax.ppermute(minus1, "seq", plus_pairs(seqs, 2))
    minus6 = lax.ppermute(minus7, "seq", minus_pairs(seqs, 2))
    minus1, later = lax.optimization_barrier((minus1, where))
    query = prepare_queries(later, doc_lengths, query_proj, query_gain.reshape(1, HD))
    minus2, query, mine = lax.optimization_barrier((minus2, query, mine))
    minus3 = lax.ppermute(minus2, "seq", plus_pairs(seqs, 3))
    minus5 = lax.ppermute(minus6, "seq", minus_pairs(seqs, 3))
    cache = lax.ppermute(mine, ("seq", "group"), slot_pairs(seqs, groups))
    minus3, kv_again = lax.optimization_barrier((minus3, kv))
    plus4 = lax.ppermute(minus3, "seq", plus_pairs(seqs, 4))
    minus4 = lax.ppermute(minus5, "seq", minus_pairs(seqs, 4))
    acc, stat = attend_early(
        (0, 1, 7, 2, 6, 3, 5),
        where,
        doc_lengths,
        query,
        [kv, minus1, minus7, minus2, minus6, minus3, minus5],
    )
    minus8 = lax.ppermute(kv_again, "seq", partner_pairs(seqs))
    attended, cache = attend_late(
        (8, 4), where, doc_lengths, query, acc, stat, cache, [minus8, plus4, minus4]
    )
    return attended, cache.reshape(1, 1, groups, 1, PAGE, 2 * HD)


def solution(mesh):
    rows = P("group", "seq", None)
    in_specs = (rows, rows, rows, P(), P(), P("group", None))
    out_specs = (rows, P("seq", "group", None, None, None, None))
    return jax.shard_map(body, mesh=mesh, in_specs=in_specs, out_specs=out_specs, check_vma=False)
```
